256 devices in a mesh: seq: 128 (over x, z, y), vocab: 2 (over core).
Axes of the slice: x: 4, y: 4, z: 8, core: 2. Of those that a mesh axis runs over, the one named last changes fastest.
Arguments:
- frames: bfloat16 [65536, 1280], P('seq', 'vocab'), may hold values from -6 to 6
- conv_weight: bfloat16 [31, 1280], P(None, 'vocab'), may hold values from -1 to 1
- proj_weight: bfloat16 [1280, 3584], P('seq', 'vocab'), may hold values from -0.15625 to 0.15625
- table: bfloat16 [152064, 3584], P('seq', 'vocab'), may hold values from -6 to 6
- audio_pos: int32 [16384], P('seq'), may hold values from 0 to 32767, as said below
- token_ids: int32 [32768], P('seq'), may hold values from 0 to 152063, as said below
- cotangent: bfloat16 [32768, 3584], P('seq', 'vocab'), may hold values from -6 to 6
Outputs:
- llm_input: bfloat16 [32768, 3584], P('seq', 'vocab')
- grad_table: bfloat16 [152064, 3584], P('seq', 'vocab')
The draws below stay inside these ranges and needn't reach their ends.
Inputs may be any that keep to these rules, and one draw needn't show every extreme that they name: `audio_pos`: the entries are distinct; with the slots not named they cover all slots once. The 128 rows of one aligned block of 128 rows take consecutive slots in order. A row held by seq device s (rows s * 128 to (s + 1) * 128 - 1) goes to a slot of s * 256 to (s + 2) * 256 - 1. For every seq device s but the last, its last held row goes to a slot of seq device s + 1. `token_ids`: seq device s holds vocabulary rows s * 1188 to (s + 1) * 1188 - 1 and slots s * 256 to (s + 1) * 256 - 1. Among the slots of one seq device at most 2 ids fall in the rows of one seq device, and in every such block of slots exactly 2 fall in the rows of some seq device.
All inputs are finite; a program needn't handle non-finite values.
Results may differ from the reference program's by a relative error of at most 0.0023.
Values may be sent and summed in bfloat16 or wider, within the bound.
A program may use at most 128 MiB of HBM per device.

```python
import jax
import jax.numpy as jnp

C = 1280
K = 31
D = 3584
V = 152064
POOL = 4
BLOCK = 128
TXT_DEV = 128
FRAMES = 65536
P_DEV = 128
AUDIO = 16384
S_DEV = 256
SLOTS = 32768
VROWS = 1188
CAP = 2
N_SEQ = 128


def draw_audio_pos(key, part):
    key = jax.random.fold_in(key, 11)
    key_drift, key_runs = jax.random.split(key)
    drift = jax.random.randint(key_drift, (N_SEQ,), 1, TXT_DEV + 1)
    drift = jnp.where(jnp.arange(N_SEQ) == N_SEQ - 1, 0, drift).astype(jnp.int32)
    earlier = jnp.concatenate([jnp.zeros((1,), jnp.int32), drift[:-1]])
    text_count = TXT_DEV + drift - earlier
    blocks = P_DEV // BLOCK
    runs = jax.random.randint(key_runs, (N_SEQ, blocks), 0, (text_count // blocks + 1)[:, None]).astype(jnp.int32)
    head_runs = runs[:, :blocks - 1]
    last_run = text_count - jnp.sum(head_runs, axis=1)
    runs = jnp.concatenate([head_runs, last_run[:, None]], axis=1)
    before = jnp.cumsum(runs, axis=1)
    unit_start = jnp.arange(N_SEQ) * S_DEV + earlier
    block_start = unit_start[:, None] + jnp.arange(blocks)[None, :] * BLOCK + before
    positions = block_start[:, :, None] + jnp.arange(BLOCK)[None, None, :]
    return positions.reshape(AUDIO).astype(jnp.int32)


def owner_block(key):
    key_heavy, key_pick, key_mix = jax.random.split(key, 3)
    heavy = jax.random.randint(key_heavy, (), 0, N_SEQ)
    picked = jax.random.permutation(key_pick, (N_SEQ - 1) * CAP)[:S_DEV - CAP] // CAP
    picked = picked + (picked >= heavy).astype(picked.dtype)
    owners = jnp.concatenate([jnp.full((CAP,), heavy, jnp.int32), picked.astype(jnp.int32)])
    return jax.random.permutation(key_mix, owners)


def draw_token_ids(key, part):
    key = jax.random.fold_in(key, 23)
    key_owner, key_row = jax.random.split(key)
    owners = jax.vmap(owner_block)(jax.random.split(key_owner, N_SEQ))
    rows = jax.random.randint(key_row, (N_SEQ, S_DEV), 0, VROWS)
    return (owners * VROWS + rows).reshape(SLOTS).astype(jnp.int32)


def block_levels(own_key, dims, cuts, low, largest):
    level = 1.0
    for axis_at, shards_of in cuts:
        draws = jax.random.uniform(jax.random.fold_in(jax.random.fold_in(own_key, 6), axis_at), (shards_of,), jnp.float32, low / len(cuts), largest / len(cuts))
        level = level * jnp.repeat(jnp.exp(draws), dims[axis_at] // shards_of).reshape((-1,) + (1,) * (len(dims) - 1 - axis_at))
    return level


def normal_values(rng, shape, scale, bound, shards=(), kind=jnp.bfloat16):
    result = scale * jax.random.normal(rng, shape, jnp.float32)
    if shards:
        result = result * block_levels(rng, shape, shards, -0.22, 0.18)
    return jnp.clip(result, -bound, bound).astype(kind)


def setup_inputs(seed: int = 0) -> dict:
    streams_of = jax.random.split(jax.random.key(seed), 8)
    frames = normal_values(streams_of[0], (FRAMES, C), 1.0, 6.0, ((0, 128), (1, 2)))
    conv_weight = normal_values(streams_of[1], (K, C), K ** -0.5, 1.0, ((1, 2),))
    proj_weight = normal_values(streams_of[2], (C, D), C ** -0.5, 0.15625, ((0, 128), (1, 2)))
    table = normal_values(streams_of[3], (V, D), 1.0, 6.0, ((0, 128), (1, 2)))
    audio_pos = draw_audio_pos(jax.random.fold_in(streams_of[7], 71), 0)
    token_ids = draw_token_ids(jax.random.fold_in(streams_of[7], 71), 0)
    cotangent = normal_values(streams_of[6], (SLOTS, D), 1.0, 6.0, ((0, 128), (1, 2)))
    return {"frames": frames, "conv_weight": conv_weight, "proj_weight": proj_weight, "table": table, "audio_pos": audio_pos, "token_ids": token_ids, "cotangent": cotangent}


def reference(frames, conv_weight, proj_weight, table, audio_pos, token_ids, cotangent):
    rim_width = (K - 1) // 2
    padded = jnp.pad(frames, ((rim_width, rim_width), (0, 0)))
    filtered = jnp.zeros((FRAMES, C), jnp.float32)
    for tap_index in range(K):
        filtered = filtered + padded[tap_index:tap_index + FRAMES].astype(jnp.float32) * conv_weight[tap_index].astype(jnp.float32)
    activated = frames.astype(jnp.float32) + jax.nn.silu(filtered)
    pooled = activated.reshape(AUDIO, POOL, C).mean(axis=1).astype(jnp.bfloat16)
    audio_rows = jnp.dot(pooled, proj_weight, preferred_element_type=jnp.float32).astype(jnp.bfloat16)
    text_rows = jnp.take(table, token_ids, axis=0)
    llm_input = text_rows.at[audio_pos].set(audio_rows)
    audio_mark = jnp.zeros((SLOTS,), jnp.float32).at[audio_pos].set(1.0)
    weighted = cotangent.astype(jnp.float32) * (1.0 - audio_mark)[:, None]
    grad_table = jnp.zeros((V, D), jnp.float32).at[token_ids].add(weighted).astype(jnp.bfloat16)
    return llm_input, grad_table
```

```python
import functools

import jax
import jax.numpy as jnp
import numpy as np
from jax import lax
from jax.experimental import pallas as pl
from jax.experimental.pallas import tpu as pltpu
from jax.sharding import PartitionSpec as P

MESH = pl.DeviceIdType.MESH
BF = jnp.bfloat16
F32 = jnp.float32
NX, NZ, NY = 4, 8, 4
N_SEQ = NX * NZ * NY
PLANE = NX * NY
POOL = 4
SLOT = 256
RUN = 128
VROWS = 1188
D = 1792
NC = 2
CW = D // NC
CH = 640
FR = 512
TAPS = 31
WROWS = 10
WP = 1152
KB = NZ * WROWS


def relay_matrix():
    m = np.zeros((SLOT, SLOT), np.float32)
    for z in range(NZ):
        for k in range(2):
            for p in range(PLANE):
                m[p * 16 + k * 8 + z, z * 32 + k * 16 + p] = 1
    return m


def channel_matrix():
    m = np.zeros((CH, CH), np.float32)
    for c in range(CH):
        x, z, y, i = c // 320, (c % 320) // 40, (c % 40) // 10, c % 10
        inner = z * 8 + i if i < 8 else 64 + z * 2 + i - 8
        m[c, (x * 4 + y) * KB + inner] = 1
    return m


def pack_matrices():
    m = np.zeros((9, 16, 16), np.float32)
    for i in range(8):
        m[0, i, i] = 1
        m[1, 8 + i, i] = 1
    for g in range(7):
        for i in range(2):
            m[2 + g, 2 * g + i, 8 + i] = 1
    return m.reshape(9 * 16, 16)


def unpack_matrices():
    top = np.zeros((2, 64, 128), np.float32)
    low = np.zeros((7, 16, 128), np.float32)
    for z in range(NZ):
        for i in range(8):
            top[0, z * 8 + i, z * 16 + i] = 1
            top[1, z * 8 + i, z * 16 + 8 + i] = 1
        for g in range(7):
            for i in range(2):
                low[g, z * 2 + i, z * 16 + 2 * g + i] = 1
    return np.concatenate([top.reshape(128, 128), low.reshape(112, 128)])


def mm(a, b):
    return jnp.dot(a, b, preferred_element_type=F32)


def comm_kernel(
    ids_ref, pos_ref, frames_ref, cw_ref, w_ref, relay_ref, back_ref, chan_ref, pack_ref, unpack_ref,
    cot_hbm, table_hbm,
    llm_hbm, got_hbm, row_ref,
    cot, table, sel_s, snd1, rcv1, snd2, rcv2, bsnd1, brcv1, bsnd2, brcv2,
    idsnd, idrcv, idcomp, idall, stsnd, strcv, halo, ext, cwf, act, pooled, plo, plp,
    wpadf, wpk, wrz, wst, wfull, xs, llm,
    loc_sem, st_sem, halo_sem, idz_s, idz_r, idp_s, idp_r, wz_s, wz_r,
    fz_s, fz_r, fp_s, fp_r, bp_s, bp_r, bz_s, bz_r,
    w1_s, w1_r, w1x_s, w1x_r, w2_s, w2_r, w2x_s, w2x_r, pool_s, pool_r,
):
    s = lax.axis_index("seq")
    v = lax.axis_index("vocab")
    x, z, y = s // 32, (s // 4) % 8, s % 4
    p = x * 4 + y

    def at(xx, zz, yy):
        return ((xx * 8 + zz) * 4 + yy, v)

    def zpeer(d):
        return at(x, lax.rem(z + d, 8), y)

    def ppeer(j):
        return at(lax.rem(x + j // 4, 4), z, lax.rem(y + lax.rem(j, 4), 4))

    def pplace(j):
        return lax.rem(x + j // 4, 4) * 4 + lax.rem(y + lax.rem(j, 4), 4)

    nxt = (lax.rem(s + 1, N_SEQ), v)
    prv = (lax.rem(s + N_SEQ - 1, N_SEQ), v)
    other = (s, 1 - v)

    def remote(src, dst, ss, rs, dev):
        return pltpu.make_async_remote_copy(
            src_ref=src, dst_ref=dst, send_sem=ss, recv_sem=rs, device_id=dev, device_id_type=MESH
        )

    bar = pltpu.get_barrier_semaphore()
    for d in range(1, 8):
        pl.semaphore_signal(bar, inc=1, device_id=zpeer(d), device_id_type=MESH)

    def greet(j, c):
        pl.semaphore_signal(bar, inc=1, device_id=ppeer(j), device_id_type=MESH)
        return c

    lax.fori_loop(1, PLANE, greet, 0)
    for dev in (nxt, prv, other):
        pl.semaphore_signal(bar, inc=1, device_id=dev, device_id_type=MESH)

    cot_cp = pltpu.make_async_copy(cot_hbm, cot, loc_sem.at[0])
    cot_cp.start()
    table_cp = pltpu.make_async_copy(table_hbm, table, loc_sem.at[1])
    table_cp.start()

    bcol = lax.broadcasted_iota(jnp.int32, (SLOT, 1), 0)
    bz, bk, bp = bcol >> 5, (bcol >> 4) & 1, bcol & 15
    low = (((bp >> 2) * 8 + bz) * 4 + (bp & 3)) * VROWS
    rel = ids_ref[...] - low
    qi = lax.broadcasted_iota(jnp.int32, (SLOT, SLOT), 1).astype(F32)
    hit = (rel >= 0) & (rel < VROWS)
    first = jnp.min(jnp.where(hit, qi, 4096.0), axis=1, keepdims=True)
    last = jnp.max(jnp.where(hit, qi, -1.0), axis=1, keepdims=True)
    chosen = jnp.where(bk == 0, first, jnp.where(last > first, last, -1.0))
    picked = qi == chosen
    sel_s[...] = jnp.where(picked, 1.0, 0.0).astype(BF)
    relf = jnp.where(picked, (rel + 1).astype(F32), 0.0)

    wpadf[...] = jnp.zeros_like(wpadf)
    wpadf[0:WROWS, :] = w_ref[...].astype(F32)
    wp = wpadf[...].astype(BF)
    half = D // 2
    wpk[:, 0:half] = (mm(pack_ref[0:16], wp[:, 0:half]) + mm(pack_ref[16:32], wp[:, half:])).astype(BF)
    tail = jnp.zeros((16, 256), F32)
    for g in range(7):
        tail = tail + mm(pack_ref[32 + 16 * g : 48 + 16 * g], wp[:, 256 * g : 256 * g + 256])
    wpk[:, half:] = tail.astype(BF)
    zrow16 = pl.multiple_of(z * 16, 16)
    wrz[pl.ds(zrow16, 16), :] = wpk[...]

    start = pos_ref[0:1, 0:1]
    stsnd[...] = jnp.broadcast_to(start, (8, 128))

    pl.semaphore_wait(bar, 7 + PLANE - 1 + 3)

    st_cp = remote(stsnd, strcv, st_sem.at[0], st_sem.at[1], nxt)
    st_cp.start()
    up_cp = remote(frames_ref.at[pl.ds(FR - 16, 16)], halo.at[0], halo_sem.at[0], halo_sem.at[1], nxt)
    dn_cp = remote(frames_ref.at[pl.ds(0, 16)], halo.at[1], halo_sem.at[2], halo_sem.at[3], prv)
    up_cp.start()
    dn_cp.start()
    wz_cps = [
        remote(wpk, wrz.at[pl.ds(zrow16, 16)], wz_s.at[d], wz_r.at[d], zpeer(d)) for d in range(1, 8)
    ]
    for cp in wz_cps:
        cp.start()

    zrow = pl.multiple_of(z * 32, 32)
    cot_cp.wait()
    fz_cps = []
    for c in range(NC):
        snd1[c] = mm(sel_s[...], cot[:, c * CW : (c + 1) * CW]).astype(BF)

    st_cp.wait()
    before = jnp.where(s > 0, strcv[0:1, 0:1], -4096)
    slot = s * SLOT + lax.broadcasted_iota(jnp.int32, (1, SLOT), 1)
    audio = ((slot >= start) & (slot < start + RUN)) | ((slot >= before) & (slot < before + RUN))
    idv = jnp.sum(jnp.where(audio, 0.0, relf), axis=1, keepdims=True) - 1.0
    brow = lax.broadcasted_iota(jnp.int32, (SLOT, SLOT), 0)
    qcol = lax.broadcasted_iota(jnp.int32, (SLOT, SLOT), 1)
    diag = brow == qcol
    idrow = jnp.sum(jnp.where(diag, idv, 0.0), axis=0, keepdims=True)
    eight = lax.broadcasted_iota(jnp.int32, (8, 128), 0)
    idsnd[...] = jnp.where(eight == 0, idrow[:, 0:128], idrow[:, 128:256]).astype(jnp.int32)
    zrow8 = pl.multiple_of(z * 8, 8)
    idrcv[pl.ds(zrow8, 8), :] = idsnd[...]
    idz_cps = [
        remote(idsnd, idrcv.at[pl.ds(zrow8, 8)], idz_s.at[d], idz_r.at[d], zpeer(d)) for d in range(1, 8)
    ]
    for cp in idz_cps:
        cp.start()

    for c in range(NC):
        for d in (1, 7, 2, 6, 3, 5, 4):
            to = pl.multiple_of(lax.rem(z + d, 8) * 32, 32)
            cp = remote(
                snd1.at[c, pl.ds(to, 32)], rcv1.at[c, pl.ds(zrow, 32)], fz_s.at[c, d], fz_r.at[c, d], zpeer(d)
            )
            cp.start()
            fz_cps.append(cp)
        rcv1[c, pl.ds(zrow, 32), :] = snd1[c, pl.ds(zrow, 32), :]

    for cp in idz_cps:
        cp.wait()
    even = idrcv[pl.ds(0, 8, stride=8), :]
    odd = idrcv[pl.ds(1, 8, stride=8), :]
    idcomp[...] = jnp.where(z < 4, even, odd)
    prow8 = pl.multiple_of(p * 8, 8)
    idall[pl.ds(prow8, 8), :] = idcomp[...]

    def idp_copy(j):
        return remote(idcomp, idall.at[pl.ds(prow8, 8)], idp_s.at[j], idp_r.at[j], ppeer(j))

    def plane(fn):
        def body(j, c):
            fn(j)
            return c

        lax.fori_loop(1, PLANE, body, 0)

    plane(lambda j: idp_copy(j).start())

    for cp in wz_cps:
        cp.wait()
    prow80 = pl.multiple_of(p * KB, 16)
    packed = wrz[...]
    for c in range(NC):
        wst[c, 0:64, :] = mm(unpack_ref[64 * c : 64 * c + 64], packed[:, 0:half]).astype(BF)
    for g in range(7):
        piece = mm(unpack_ref[128 + 16 * g : 144 + 16 * g], packed[:, half:]).astype(BF)
        for b in range(2):
            col = 256 * g + 128 * b
            c, off = col // CW, col % CW
            wst[c, 64:KB, off : off + 128] = piece[:, 128 * b : 128 * b + 128]

    for c in range(NC):
        wfull[c, pl.ds(prow80, KB), :] = wst[c]

    def wplace(c, f, g):
        ff, gg = lax.rem((x if c == 0 else y) + f, 4), lax.rem((y if c == 0 else x) + g, 4)
        return ff * 4 + gg if c == 0 else gg * 4 + ff

    def wpeer(c, f, g):
        ff, gg = lax.rem((x if c == 0 else y) + f, 4), lax.rem((y if c == 0 else x) + g, 4)
        return at(ff, z, gg) if c == 0 else at(gg, z, ff)

    def wblock(c, f, g, lo=0, n=KB):
        return wfull.at[c, pl.ds(pl.multiple_of(wplace(c, f, g) * KB + lo, 16), n)]

    def wsend(c, block, sems, dev):
        cp = remote(block, block, sems[0], sems[1], dev)
        cp.start()
        return cp

    wsends = []

    for c in range(NC):
        for i, f in enumerate((1, 3)):
            wsends.append(wsend(c, wblock(c, 0, 0), (w1_s.at[c, i], w1_r.at[c, i]), wpeer(c, f, 0)))
    for c in range(NC):
        for i, g in enumerate((1, 3)):
            wsends.append(wsend(c, wblock(c, 0, 0), (w2_s.at[c, i, 0], w2_r.at[c, i, 0]), wpeer(c, 0, g)))

    def wgot(block, sem):
        remote(block, block, w1_s.at[0, 0], sem, other).wait_recv()

    plane(lambda j: idp_copy(j).wait())
    dup = []
    for i in range(PLANE):
        piece = idall[8 * i : 8 * i + 8, :]
        dup += [piece, piece]
    every = jnp.concatenate(dup, axis=0)
    lane = lax.broadcasted_iota(jnp.int32, (SLOT, 128), 1)
    rrow = lax.broadcasted_iota(jnp.int32, (SLOT, 128), 0)
    want = lax.rem(z, 4) * 32 + ((rrow >> 3) & 1) * 16 + p
    rowid = jnp.sum(jnp.where(lane == want, every, 0).astype(F32), axis=1, keepdims=True)
    row_ref[...] = jnp.broadcast_to(
        jnp.sum(jnp.where(diag, rowid, 0.0), axis=0, keepdims=True).astype(jnp.int32), (8, SLOT)
    )
    vi = lax.broadcasted_iota(jnp.int32, (SLOT, VROWS), 1)
    look = jnp.where(vi == rowid.astype(jnp.int32), 1.0, 0.0).astype(BF)
    table_cp.wait()
    prow16 = pl.multiple_of(p * 16, 16)

    def bp_copy(c, j):
        to = pl.multiple_of(pplace(j) * 16, 16)
        return remote(
            bsnd1.at[c, pl.ds(to, 16)], brcv1.at[c, pl.ds(prow16, 16)], bp_s.at[c, j], bp_r.at[c, j], ppeer(j)
        )

    for c in range(NC):
        bsnd1[c] = mm(look, table[:, c * CW : (c + 1) * CW]).astype(BF)
        plane(lambda j: bp_copy(c, j).start())
        brcv1[c, pl.ds(prow16, 16), :] = bsnd1[c, pl.ds(prow16, 16), :]

    for c in range(NC):
        wgot(wblock(c, 3, 0), w1_r.at[c, 0])
        wsends.append(wsend(c, wblock(c, 3, 0, 0, 48), (w1x_s.at[c, 0], w1x_r.at[c, 0]), wpeer(c, 1, 0)))
        wgot(wblock(c, 1, 0), w1_r.at[c, 1])
        wsends.append(wsend(c, wblock(c, 1, 0, 48, 32), (w1x_s.at[c, 1], w1x_r.at[c, 1]), wpeer(c, 3, 0)))
        for f in (1, 3):
            for i, g in enumerate((1, 3)):
                wsends.append(wsend(c, wblock(c, f, 0), (w2_s.at[c, i, f], w2_r.at[c, i, f]), wpeer(c, 0, g)))

    up_cp.wait()
    dn_cp.wait()
    for l in range(5):
        cols = slice(128 * l, 128 * l + 128)
        ext[l, 16 : 16 + FR, :] = frames_ref[:, cols].astype(F32)
        ext[l, 0:16, :] = jnp.where(s > 0, halo[0, :, cols].astype(F32), 0.0)
        ext[l, 16 + FR : 32 + FR, :] = jnp.where(s < N_SEQ - 1, halo[1, :, cols].astype(F32), 0.0)
        cwf[l, 0:TAPS, :] = cw_ref[:, cols].astype(F32)

    def conv(i, carry):
        l, rb = i // 8, lax.rem(i, 8)
        r0 = pl.multiple_of(rb * 64, 64)
        acc = jnp.zeros((64, 128), F32)
        for j in range(TAPS):
            acc = acc + ext[l, pl.ds(r0 + (j + 1), 64), :] * cwf[l, pl.ds(j, 1), :]
        act[...] = ext[l, pl.ds(r0 + 16, 64), :] + acc / (1.0 + jnp.exp(-acc))
        total = act[pl.ds(0, 16, stride=4), :]
        for k in range(1, POOL):
            total = total + act[pl.ds(k, 16, stride=4), :]
        pooled[pl.ds(pl.multiple_of(rb * 16, 16), 16), pl.ds(pl.multiple_of(l * 128, 128), 128)] = (
            total * (1.0 / POOL)
        ).astype(BF)
        return carry

    lax.fori_loop(0, 40, conv, 0)
    plo[v] = mm(pooled[...], chan_ref[...]).astype(BF)
    core_cp = remote(plo.at[v], plo.at[v], pool_s.at[0], pool_r.at[0], other)
    next_cp = remote(plo.at[v], plp.at[v], pool_s.at[1], pool_r.at[1], nxt)
    core_cp.start()
    next_cp.start()

    def fp_copy(c, j):
        to = pl.multiple_of(pplace(j) * 16, 16)
        return remote(
            snd2.at[c, pl.ds(to, 16)], rcv2.at[c, pl.ds(prow16, 16)], fp_s.at[c, j], fp_r.at[c, j], ppeer(j)
        )

    def forward(c):
        for cp in fz_cps[7 * c : 7 * c + 7]:
            cp.wait()
        snd2[c] = mm(relay_ref[...], rcv1[c]).astype(BF)
        plane(lambda j: fp_copy(c, j).start())
        rcv2[c, pl.ds(prow16, 16), :] = snd2[c, pl.ds(prow16, 16), :]

    bz_cps = []

    def back(c):
        plane(lambda j: bp_copy(c, j).wait())
        bsnd2[c] = mm(back_ref[...], brcv1[c]).astype(BF)
        for d in (1, 7, 2, 6, 3, 5, 4):
            to = pl.multiple_of(lax.rem(z + d, 8) * 32, 32)
            cp = remote(
                bsnd2.at[c, pl.ds(to, 32)], brcv2.at[c, pl.ds(zrow, 32)], bz_s.at[c, d], bz_r.at[c, d], zpeer(d)
            )
            cp.start()
            bz_cps.append(cp)
        brcv2[c, pl.ds(zrow, 32), :] = bsnd2[c, pl.ds(zrow, 32), :]

    back(0)
    back(1)

    for c in range(NC):
        wgot(wblock(c, 2, 0, 0, 48), w1x_r.at[c, 0])
        wgot(wblock(c, 2, 0, 48, 32), w1x_r.at[c, 1])
        for i, g in enumerate((1, 3)):
            wsends.append(wsend(c, wblock(c, 2, 0), (w2_s.at[c, i, 2], w2_r.at[c, i, 2]), wpeer(c, 0, g)))

    def w2relay(c, f):
        i, near, to = (0, 3, 1) if f < 2 else (1, 1, 3)
        wgot(wblock(c, f, near), w2_r.at[c, i, f])
        wsends.append(wsend(c, wblock(c, f, near), (w2x_s.at[c, f], w2x_r.at[c, f]), wpeer(c, 0, to)))

    for c in range(NC):
        w2relay(c, 0)

    forward(0)

    for f in (1, 3, 2):
        for c in range(NC):
            w2relay(c, f)

    forward(1)

    next_cp.wait()
    fwd_cp = remote(plp.at[v], plp.at[v], pool_s.at[2], pool_r.at[2], other)
    fwd_cp.start()
    core_cp.wait()
    fwd_cp.wait()
    qslot = s * SLOT + lax.broadcasted_iota(jnp.int32, (SLOT, RUN), 0)
    prun = lax.broadcasted_iota(jnp.int32, (SLOT, RUN), 1)
    own_sel = jnp.where(qslot == start + prun, 1.0, 0.0).astype(BF)
    prev_sel = jnp.where(qslot == before + prun, 1.0, 0.0).astype(BF)
    for h in range(2):
        xs[:, h * CH : (h + 1) * CH] = (mm(own_sel, plo[h]) + mm(prev_sel, plp[h])).astype(BF)

    for c in range(NC):
        for f in range(4):
            i, near = (1, 1) if f < 2 else (0, 3)
            wgot(wblock(c, f, near), w2_r.at[c, i, f])
            wgot(wblock(c, f, 2), w2x_r.at[c, f])
        llm[c] = mm(xs[...], wfull[c]).astype(BF)

    outs = []
    for c in range(NC):
        plane(lambda j: fp_copy(c, j).wait())
        cp = pltpu.make_async_copy(rcv2.at[c], got_hbm.at[:, pl.ds(c * CW, CW)], loc_sem.at[2 + c])
        cp.start()
        outs.append(cp)
    for c in range(NC):
        for cp in bz_cps[7 * c : 7 * c + 7]:
            cp.wait()
        text = lax.dot_general(sel_s[...], brcv2[c], (((0,), (0,)), ((), ())), preferred_element_type=F32)
        llm[c] = (text + llm[c].astype(F32)).astype(BF)
        cp = pltpu.make_async_copy(llm.at[c], llm_hbm.at[:, pl.ds(c * CW, CW)], loc_sem.at[4 + c])
        cp.start()
        outs.append(cp)
    for cp in wsends:
        cp.wait_send()
    for cp in outs:
        cp.wait()


def out_kernel(row_ref, got_ref, llm_ref, out_ref, grad_ref, place):
    @pl.when(pl.program_id(0) == 0)
    def _():
        vi = lax.broadcasted_iota(jnp.int32, (VROWS, SLOT), 0)
        place[...] = jnp.where(vi == row_ref[0:1, :], 1.0, 0.0).astype(BF)

    grad_ref[...] = mm(place[...], got_ref[...]).astype(BF)
    out_ref[...] = llm_ref[...]


def shards(frames, conv_weight, proj_weight, table, audio_pos, token_ids, cotangent):
    relay = relay_matrix()
    consts = [relay, relay.T, channel_matrix(), pack_matrices(), unpack_matrices()]
    consts = [jnp.asarray(m, dtype=BF) for m in consts]
    vm = pl.BlockSpec(memory_space=pltpu.VMEM)
    hbm = pl.BlockSpec(memory_space=pl.ANY)
    dma = pltpu.SemaphoreType.DMA
    wide = pltpu.VMEM((NC, SLOT, CW), BF)
    llm, got, rows = pl.pallas_call(
        comm_kernel,
        out_shape=[
            jax.ShapeDtypeStruct((SLOT, D), BF),
            jax.ShapeDtypeStruct((SLOT, D), BF),
            jax.ShapeDtypeStruct((8, SLOT), jnp.int32),
        ],
        in_specs=[vm] * 10 + [hbm] * 2,
        out_specs=[hbm, hbm, vm],
        scratch_shapes=[
            pltpu.VMEM((SLOT, D), BF),
            pltpu.VMEM((VROWS, D), BF),
            pltpu.VMEM((SLOT, SLOT), BF),
            wide, wide, wide, wide, wide, wide, wide, wide,
            pltpu.VMEM((8, 128), jnp.int32),
            pltpu.VMEM((64, 128), jnp.int32),
            pltpu.VMEM((8, 128), jnp.int32),
            pltpu.VMEM((128, 128), jnp.int32),
            pltpu.VMEM((8, 128), jnp.int32),
            pltpu.VMEM((8, 128), jnp.int32),
            pltpu.VMEM((2, 16, CH), BF),
            pltpu.VMEM((5, FR + 32, 128), F32),
            pltpu.VMEM((5, 32, 128), F32),
            pltpu.VMEM((64, 128), F32),
            pltpu.VMEM((RUN, CH), BF),
            pltpu.VMEM((2, RUN, CH), BF),
            pltpu.VMEM((2, RUN, CH), BF),
            pltpu.VMEM((16, D), F32),
            pltpu.VMEM((16, WP), BF),
            pltpu.VMEM((128, WP), BF),
            pltpu.VMEM((NC, KB, CW), BF),
            pltpu.VMEM((NC, PLANE * KB, CW), BF),
            pltpu.VMEM((SLOT, 2 * CH), BF),
            wide,
            dma((6,)), dma((2,)), dma((4,)),
            dma((8,)), dma((8,)), dma((16,)), dma((16,)), dma((8,)), dma((8,)),
            dma((2, 8)), dma((2, 8)), dma((2, 16)), dma((2, 16)),
            dma((2, 16)), dma((2, 16)), dma((2, 8)), dma((2, 8)),
            dma((2, 2)), dma((2, 2)), dma((2, 2)), dma((2, 2)),
            dma((2, 2, 4)), dma((2, 2, 4)), dma((2, 4)), dma((2, 4)),
            dma((3,)), dma((3,)),
        ],
        compiler_params=pltpu.CompilerParams(
            collective_id=0, has_side_effects=True, vmem_limit_bytes=48 * 1024 * 1024
        ),
        name="exchange",
    )(
        token_ids.reshape(1, SLOT), audio_pos.reshape(1, RUN), frames, conv_weight, proj_weight, *consts,
        cotangent, table,
    )
    tile = 256
    return pl.pallas_call(
        out_kernel,
        grid=(D // tile,),
        out_shape=[jax.ShapeDtypeStruct((SLOT, D), BF), jax.ShapeDtypeStruct((VROWS, D), BF)],
        in_specs=[
            pl.BlockSpec((8, SLOT), lambda i: (0, 0)),
            pl.BlockSpec((SLOT, tile), lambda i: (0, i)),
            pl.BlockSpec((SLOT, tile), lambda i: (0, i)),
        ],
        out_specs=[
            pl.BlockSpec((SLOT, tile), lambda i: (0, i)),
            pl.BlockSpec((VROWS, tile), lambda i: (0, i)),
        ],
        scratch_shapes=[pltpu.VMEM((VROWS, SLOT), BF)],
        compiler_params=pltpu.CompilerParams(vmem_limit_bytes=24 * 1024 * 1024),
        name="write",
    )(rows, got, llm)


def solution(mesh):
    return jax.shard_map(
        shards,
        mesh=mesh,
        in_specs=(
            P("seq", "vocab"),
            P(None, "vocab"),
            P("seq", "vocab"),
            P("seq", "vocab"),
            P("seq"),
            P("seq"),
            P("seq", "vocab"),
        ),
        out_specs=(P("seq", "vocab"), P("seq", "vocab")),
        check_vma=False,
    )
```

```python
import functools

import jax
import jax.numpy as jnp
import numpy as np
from jax import lax
from jax.experimental import pallas as pl
from jax.experimental.pallas import tpu as pltpu
from jax.sharding import PartitionSpec as P

MESH = pl.DeviceIdType.MESH
BF = jnp.bfloat16
F32 = jnp.float32
NX, NZ, NY = 4, 8, 4
N_SEQ = NX * NZ * NY
PLANE = NX * NY
POOL = 4
SLOT = 256
RUN = 128
VROWS = 1188
D = 1792
NC = 2
CW = D // NC
CH = 640
FR = 512
TAPS = 31
WROWS = 10
WP = 1152
KB = NZ * WROWS
TILE = 256
VMEM_LIMIT = 60 * 1024 * 1024


def relay_matrix():
    m = np.zeros((SLOT, SLOT), np.float32)
    for z in range(NZ):
        for k in range(2):
            for p in range(PLANE):
                m[p * 16 + k * 8 + z, z * 32 + k * 16 + p] = 1
    return m


def channel_matrix():
    m = np.zeros((CH, CH), np.float32)
    for c in range(CH):
        x, z, y, i = c // 320, (c % 320) // 40, (c % 40) // 10, c % 10
        inner = z * 8 + i if i < 8 else 64 + z * 2 + i - 8
        m[c, (x * 4 + y) * KB + inner] = 1
    return m


def pack_matrices():
    m = np.zeros((9, 16, 16), np.float32)
    for i in range(8):
        m[0, i, i] = 1
        m[1, 8 + i, i] = 1
    for g in range(7):
        for i in range(2):
            m[2 + g, 2 * g + i, 8 + i] = 1
    return m.reshape(9 * 16, 16)


def unpack_matrices():
    top = np.zeros((2, 64, 128), np.float32)
    low = np.zeros((7, 16, 128), np.float32)
    for z in range(NZ):
        for i in range(8):
            top[0, z * 8 + i, z * 16 + i] = 1
            top[1, z * 8 + i, z * 16 + 8 + i] = 1
        for g in range(7):
            for i in range(2):
                low[g, z * 2 + i, z * 16 + 2 * g + i] = 1
    return np.concatenate([top.reshape(128, 128), low.reshape(112, 128)])


def mm(a, b):
    return jnp.dot(a, b, preferred_element_type=F32)


def comm_kernel(
    ids_hbm, pos_hbm, frames_hbm, cw_hbm, w_hbm, relay_hbm, back_hbm, chan_hbm, pack_hbm, unpack_hbm,
    cot_hbm, table_hbm,
    llm_out, got_out, row_ref,
    ids_ref, pos_ref, frames, cw, wown, relay, backm, chan, pack, unpack,
    cot, table, sel_s, f_a, f_b, f_c, f_d, r_a, r_b, r_c, r_d,
    idsnd, idrcv, idcomp, idall, halo, ext, cwf, act, pooled, plo, plp,
    wpadf, wpk, wrz, wst, wfull, xs, far, opp, text, llm,
    loc_sem, halo_sem, idz_sem, idp_sem, wz_sem,
    f1_sem, f2_sem, r1_sem, r2_sem,
    ws_sem, w1_sem, wr_sem, wl_sem, pool_s, pool_r, xx_sem, xo_sem,
):
    s = lax.axis_index("seq")
    v = lax.axis_index("vocab")
    x, z, y = s // 32, (s // 4) % 8, s % 4
    p = x * 4 + y

    def at(xx, zz, yy):
        return ((xx * 8 + zz) * 4 + yy, v)

    def zpeer(d):
        return at(x, lax.rem(z + d, 8), y)

    def ppeer(j):
        return at(lax.rem(x + j // 4, 4), z, lax.rem(y + lax.rem(j, 4), 4))

    def pplace(j):
        return lax.rem(x + j // 4, 4) * 4 + lax.rem(y + lax.rem(j, 4), 4)

    nxt = (lax.rem(s + 1, N_SEQ), v)
    prv = (lax.rem(s + N_SEQ - 1, N_SEQ), v)
    other = (s, 1 - v)

    def remote(src, dst, ss, rs, dev):
        return pltpu.make_async_remote_copy(
            src_ref=src, dst_ref=dst, send_sem=ss, recv_sem=rs, device_id=dev, device_id_type=MESH
        )

    def wait_all(block, ss, rs):
        cp = remote(block, block, ss, rs, other)
        cp.wait_send()
        cp.wait_recv()

    def wait_got(block, rs):
        remote(block, block, ws_sem.at[0], rs, other).wait_recv()

    def plane(fn):
        def body(j, c):
            fn(j)
            return c

        lax.fori_loop(1, PLANE, body, 0)

    prow16 = pl.multiple_of(p * 16, 16)
    zrow = pl.multiple_of(z * 32, 32)

    def z_send(src, dst, sem, c):
        for d in (4, 3, 5, 2, 6, 1, 7):
            to = pl.multiple_of(lax.rem(z + d, 8) * 32, 32)
            remote(src.at[c, pl.ds(to, 32)], dst.at[c, pl.ds(zrow, 32)], sem.at[0, c], sem.at[1, c], zpeer(d)).start()
        dst[c, pl.ds(zrow, 32), :] = src[c, pl.ds(zrow, 32), :]

    def p_send(src, dst, sem, c):
        def send(j):
            to = pl.multiple_of(pplace(j) * 16, 16)
            remote(src.at[c, pl.ds(to, 16)], dst.at[c, pl.ds(prow16, 16)], sem.at[0, c], sem.at[1, c], ppeer(j)).start()

        plane(send)
        dst[c, pl.ds(prow16, 16), :] = src[c, pl.ds(prow16, 16), :]

    def z_wait(dst, sem, c):
        wait_all(dst.at[c, pl.ds(0, 224)], sem.at[0, c], sem.at[1, c])

    def p_wait(dst, sem, c):
        wait_all(dst.at[c, pl.ds(0, 240)], sem.at[0, c], sem.at[1, c])

    def turn(first, mid, last, sem1, sem2, c):
        p_wait(first, sem1, c)
        mid[c] = mm(backm[...], first[c]).astype(BF)
        z_send(mid, last, sem2, c)

    bar = pltpu.get_barrier_semaphore()
    for d in range(1, 8):
        pl.semaphore_signal(bar, inc=1, device_id=zpeer(d), device_id_type=MESH)
    plane(lambda j: pl.semaphore_signal(bar, inc=1, device_id=ppeer(j), device_id_type=MESH))
    for dev in (nxt, prv, other):
        pl.semaphore_signal(bar, inc=1, device_id=dev, device_id_type=MESH)

    local = {}
    for i, (name, src, dst) in enumerate(
        (
            ("ids", ids_hbm, ids_ref), ("pos", pos_hbm, pos_ref), ("w", w_hbm, wown), ("pack", pack_hbm, pack),
            ("frames", frames_hbm, frames), ("cot", cot_hbm, cot), ("relay", relay_hbm, relay), ("cw", cw_hbm, cw),
            ("unpack", unpack_hbm, unpack), ("back", back_hbm, backm), ("table", table_hbm, table),
            ("chan", chan_hbm, chan),
        )
    ):
        local[name] = pltpu.make_async_copy(src, dst, loc_sem.at[i])
        local[name].start()

    local["ids"].wait()
    local["pos"].wait()
    bcol = lax.broadcasted_iota(jnp.int32, (SLOT, 1), 0)
    bz, bk, bp = bcol >> 5, (bcol >> 4) & 1, bcol & 15
    low = (((bp >> 2) * 8 + bz) * 4 + (bp & 3)) * VROWS
    rel = ids_ref[...] - low
    qint = lax.broadcasted_iota(jnp.int32, (SLOT, SLOT), 1)
    qi = qint.astype(F32)
    hit = (rel >= 0) & (rel < VROWS)
    first = jnp.min(jnp.where(hit, qi, 4096.0), axis=1, keepdims=True)
    last = jnp.max(jnp.where(hit, qi, -1.0), axis=1, keepdims=True)
    chosen = jnp.where(bk == 0, first, jnp.where(last > first, last, -1.0))
    picked = qi == chosen
    sel_s[...] = jnp.where(picked, 1.0, 0.0).astype(BF)
    code = jnp.sum(jnp.where(picked, (qint * 2048 + rel + 1).astype(F32), 0.0), axis=1, keepdims=True)
    brow = lax.broadcasted_iota(jnp.int32, (SLOT, SLOT), 0)
    diag = brow == qint
    coderow = jnp.sum(jnp.where(diag, code, 0.0), axis=0, keepdims=True).astype(jnp.int32)
    start = pos_ref[0:1, 0:1]
    eight = lax.broadcasted_iota(jnp.int32, (8, 128), 0)
    idsnd[...] = jnp.where(
        eight == 0, coderow[:, 0:128], jnp.where(eight == 1, coderow[:, 128:256], jnp.broadcast_to(start, (8, 128)))
    )
    zrow8 = pl.multiple_of(z * 8, 8)
    idrcv[pl.ds(zrow8, 8), :] = idsnd[...]

    pl.semaphore_wait(bar, 7 + PLANE - 1 + 3)

    for d in (1, 7, 2, 6, 3, 5, 4):
        remote(idsnd, idrcv.at[pl.ds(zrow8, 8)], idz_sem.at[0], idz_sem.at[1], zpeer(d)).start()
    local["frames"].wait()
    remote(frames.at[pl.ds(FR - 16, 16)], halo.at[0], halo_sem.at[0], halo_sem.at[1], nxt).start()
    remote(frames.at[pl.ds(0, 16)], halo.at[1], halo_sem.at[0], halo_sem.at[1], prv).start()
    local["w"].wait()
    local["pack"].wait()
    wpadf[...] = jnp.zeros_like(wpadf)
    wpadf[0:WROWS, :] = wown[...].astype(F32)
    wp = wpadf[...].astype(BF)
    half = D // 2
    wpk[:, 0:half] = (mm(pack[0:16], wp[:, 0:half]) + mm(pack[16:32], wp[:, half:])).astype(BF)
    tail = jnp.zeros((16, 256), F32)
    for g in range(7):
        tail = tail + mm(pack[32 + 16 * g : 48 + 16 * g], wp[:, 256 * g : 256 * g + 256])
    wpk[:, half:] = tail.astype(BF)
    zrow16 = pl.multiple_of(z * 16, 16)
    wrz[pl.ds(zrow16, 16), :] = wpk[...]

    for d in (4, 3, 5, 2, 6, 1, 7):
        remote(wpk, wrz.at[pl.ds(zrow16, 16)], wz_sem.at[0], wz_sem.at[1], zpeer(d)).start()
    local["cot"].wait()
    local["relay"].wait()
    for c in range(NC):
        f_a[c] = mm(relay[...], mm(sel_s[...], cot[:, c * CW : (c + 1) * CW]).astype(BF)).astype(BF)
        if c == 0:
            p_send(f_a, f_b, f1_sem, 0)
    for name in ("cw", "unpack", "back", "table", "chan"):
        local[name].wait()

    wait_all(idrcv.at[pl.ds(0, 56)], idz_sem.at[0], idz_sem.at[1])
    even = idrcv[pl.ds(0, 8, stride=8), :]
    odd = idrcv[pl.ds(1, 8, stride=8), :]
    idcomp[0:8, :] = jnp.where(z < 4, even, odd)
    idcomp[8:16, :] = idrcv[pl.ds(2, 8, stride=8), :]
    idall[pl.ds(prow16, 16), :] = idcomp[...]
    plane(
        lambda j: remote(idcomp, idall.at[pl.ds(prow16, 16)], idp_sem.at[0], idp_sem.at[1], ppeer(j)).start()
    )
    p_send(f_a, f_b, f1_sem, 1)

    wait_all(halo, halo_sem.at[0], halo_sem.at[1])
    for l in range(5):
        cols = slice(128 * l, 128 * l + 128)
        ext[l, 16 : 16 + FR, :] = frames[:, cols].astype(F32)
        ext[l, 0:16, :] = jnp.where(s > 0, halo[0, :, cols].astype(F32), 0.0)
        ext[l, 16 + FR : 32 + FR, :] = jnp.where(s < N_SEQ - 1, halo[1, :, cols].astype(F32), 0.0)
        cwf[l, 0:TAPS, :] = cw[:, cols].astype(F32)

    def conv(i, carry):
        l, rb = i // 8, lax.rem(i, 8)
        r0 = pl.multiple_of(rb * 64, 64)
        acc = jnp.zeros((64, 128), F32)
        for j in range(TAPS):
            acc = acc + ext[l, pl.ds(r0 + (j + 1), 64), :] * cwf[l, pl.ds(j, 1), :]
        act[...] = ext[l, pl.ds(r0 + 16, 64), :] + acc / (1.0 + jnp.exp(-acc))
        total = act[pl.ds(0, 16, stride=4), :]
        for k in range(1, POOL):
            total = total + act[pl.ds(k, 16, stride=4), :]
        pooled[pl.ds(pl.multiple_of(rb * 16, 16), 16), pl.ds(pl.multiple_of(l * 128, 128), 128)] = (
            total * (1.0 / POOL)
        ).astype(BF)
        return carry

    lax.fori_loop(0, 20, conv, 0)

    turn(f_b, f_c, f_d, f1_sem, f2_sem, 0)
    lax.fori_loop(20, 40, conv, 0)
    plo[v] = mm(pooled[...], chan[...]).astype(BF)
    core_cp = remote(plo.at[v], plo.at[v], pool_s.at[0], pool_r.at[0], other)
    next_cp = remote(plo.at[v], plp.at[v], pool_s.at[1], pool_r.at[1], nxt)
    core_cp.start()
    next_cp.start()

    wait_all(wrz.at[pl.ds(0, 112)], wz_sem.at[0], wz_sem.at[1])
    prow80 = pl.multiple_of(p * KB, 16)
    packed = wrz[...]
    for c in range(NC):
        wst[c, 0:64, :] = mm(unpack[64 * c : 64 * c + 64], packed[:, 0:half]).astype(BF)
    for g in range(7):
        piece = mm(unpack[128 + 16 * g : 144 + 16 * g], packed[:, half:]).astype(BF)
        for b in range(2):
            col = 256 * g + 128 * b
            c, off = col // CW, col % CW
            wst[c, 64:KB, off : off + 128] = piece[:, 128 * b : 128 * b + 128]
    mine = lax.rem(x, 2)
    wfull[pl.ds(prow80, KB), :] = wst[mine]

    def wblock(f, g):
        return wfull.at[pl.ds(pl.multiple_of((lax.rem(x + f, 4) * 4 + lax.rem(y + g, 4)) * KB, 16), KB)]

    def wsend(block, dst, sem, dev):
        remote(block, dst, ws_sem.at[0], sem, dev).start()

    def wsecond(f):
        up, down = (wr_sem.at[f], wl_sem.at[0]) if f < 2 else (wl_sem.at[0], wr_sem.at[f])
        wsend(wblock(f, 0), wblock(f, 0), up, at(x, z, lax.rem(y + 1, 4)))
        wsend(wblock(f, 0), wblock(f, 0), down, at(x, z, lax.rem(y + 3, 4)))

    def w2relay(f):
        near, to = (3, 1) if f < 2 else (1, 3)
        wait_got(wblock(f, near), wr_sem.at[f])
        wsend(wblock(f, near), wblock(f, near), wl_sem.at[0], at(x, z, lax.rem(y + to, 4)))

    def xpeer(f):
        return at(lax.rem(x + f, 4), z, y)

    for f in (1, 3, 2):
        wsend(wst.at[mine if f == 2 else 1 - mine], wblock(0, 0), w1_sem.at[f], xpeer(f))
    wsecond(0)

    wait_all(idall.at[pl.ds(0, 240)], idp_sem.at[0], idp_sem.at[1])
    dup, dupst, sts = [], [], []
    for i in range(PLANE):
        piece, stp = idall[16 * i : 16 * i + 8, :], idall[16 * i + 8 : 16 * i + 16, :]
        dup += [piece, piece]
        dupst += [stp, stp]
        sts.append(stp)
    every = jnp.concatenate(dup, axis=0)
    lane = lax.broadcasted_iota(jnp.int32, (SLOT, 128), 1)
    rrow = lax.broadcasted_iota(jnp.int32, (SLOT, 128), 0)
    want = lax.rem(z, 4) * 32 + ((rrow >> 3) & 1) * 16 + p
    codes = jnp.sum(jnp.where(lane == want, every, 0).astype(F32), axis=1, keepdims=True).astype(jnp.int32)
    starts = jnp.concatenate(dupst, axis=0)[:, 0:1]
    mrow = lax.broadcasted_iota(jnp.int32, (128, 128), 0)
    mcol = lax.broadcasted_iota(jnp.int32, (128, 128), 1)
    strow = jnp.sum(
        jnp.where(mrow == mcol, jnp.concatenate(sts, axis=0).astype(F32), 0.0), axis=0, keepdims=True
    )
    rcol = lax.broadcasted_iota(jnp.int32, (SLOT, 1), 0)
    rp = rcol >> 4
    rs = ((rp >> 2) * 8 + (rcol & 7)) * 4 + (rp & 3)
    rprev = rs - 1
    prevm = jnp.where(rs == 0, -1, ((rprev >> 5) * 4 + (rprev & 3)) * 8 + ((rprev >> 2) & 7))
    prevst = jnp.sum(jnp.where(lane == prevm, strow, 0.0), axis=1, keepdims=True).astype(jnp.int32)
    prevst = jnp.where(rs == 0, -4096, prevst)
    rslot = rs * SLOT + (codes >> 11)
    audio = ((rslot >= starts) & (rslot < starts + RUN)) | ((rslot >= prevst) & (rslot < prevst + RUN))
    rowid = jnp.where(audio | (codes == 0), -1, (codes & 2047) - 1)
    vi = lax.broadcasted_iota(jnp.int32, (SLOT, VROWS), 1)
    look = jnp.where(vi == rowid, 1.0, 0.0).astype(BF)

    r_a[0] = mm(look, table[:, 0:CW]).astype(BF)
    p_send(r_a, r_b, r1_sem, 0)
    r_a[1] = mm(look, table[:, CW:]).astype(BF)

    rowrow = jnp.sum(jnp.where(diag, rowid.astype(F32), 0.0), axis=0, keepdims=True).astype(jnp.int32)
    sprev = lax.rem(s + N_SEQ - 1, N_SEQ)
    mprev = ((sprev // 32) * 4 + lax.rem(sprev, 4)) * 8 + lax.rem(sprev // 4, 8)
    mlane = lax.broadcasted_iota(jnp.int32, (1, 128), 1)
    before = jnp.sum(jnp.where(mlane == mprev, strow, 0.0), axis=1, keepdims=True).astype(jnp.int32)
    before = jnp.where(s > 0, before, -4096)

    turn(f_b, f_c, f_d, f1_sem, f2_sem, 1)
    for f in (1, 3, 2):
        wait_got(wblock(f, 0), w1_sem.at[4 - f])
        wsecond(f)

    p_send(r_a, r_b, r1_sem, 1)
    turn(r_b, r_c, r_d, r1_sem, r2_sem, 0)
    next_cp.wait()
    fwd_cp = remote(plp.at[v], plp.at[v], pool_s.at[2], pool_r.at[2], other)
    fwd_cp.start()
    w2relay(0)

    core_cp.wait()
    fwd_cp.wait()
    def xsend(src, dst, sem, f):
        remote(src, dst, sem.at[0], sem.at[1], xpeer(f)).start()

    qslot = s * SLOT + lax.broadcasted_iota(jnp.int32, (SLOT, RUN), 0)
    prun = lax.broadcasted_iota(jnp.int32, (SLOT, RUN), 1)
    own_sel = jnp.where(qslot == start + prun, 1.0, 0.0).astype(BF)
    prev_sel = jnp.where(qslot == before + prun, 1.0, 0.0).astype(BF)
    for h in range(2):
        xs[h, 0:SLOT, :] = (mm(own_sel, plo[h]) + mm(prev_sel, plp[h])).astype(BF)
    xsend(xs.at[v, pl.ds(0, RUN)], xs.at[v, pl.ds(SLOT, RUN)], xx_sem, 1)
    xsend(xs.at[v, pl.ds(RUN, RUN)], xs.at[v, pl.ds(SLOT + RUN, RUN)], xx_sem, 3)

    turn(r_b, r_c, r_d, r1_sem, r2_sem, 1)
    for f in (1, 3, 2):
        w2relay(f)

    wait_all(xs.at[v, pl.ds(SLOT, SLOT)], xx_sem.at[0], xx_sem.at[1])
    x_cp = remote(xs.at[v, pl.ds(SLOT, SLOT)], xs.at[v, pl.ds(SLOT, SLOT)], pool_s.at[3], pool_r.at[3], other)
    x_cp.start()

    for c in range(NC):
        z_wait(f_d, f2_sem, c)
    got_cps = []
    for c in range(NC):
        f_c[c] = mm(relay[...], f_d[c]).astype(BF)
        got_cps.append(pltpu.make_async_copy(f_c.at[c], got_out.at[:, pl.ds(c * CW, CW)], loc_sem.at[2 + c]))
        got_cps[-1].start()
    row_ref[...] = jnp.broadcast_to(rowrow, (8, SLOT))
    x_cp.wait()
    wait_got(wfull.at[pl.ds(0, 8 * KB)], wl_sem.at[0])
    far[...] = (mm(xs[0, SLOT:, :], wfull[0:CH, :]) + mm(xs[1, SLOT:, :], wfull[CH:, :])).astype(BF)
    xsend(far.at[pl.ds(0, RUN)], opp.at[pl.ds(0, RUN)], xo_sem, 3)
    xsend(far.at[pl.ds(RUN, RUN)], opp.at[pl.ds(RUN, RUN)], xo_sem, 1)
    near = mm(xs[0, 0:SLOT, :], wfull[0:CH, :]) + mm(xs[1, 0:SLOT, :], wfull[CH:, :])
    near = near.astype(BF).astype(F32)
    for c in range(NC):
        z_wait(r_d, r2_sem, c)
        text[c] = lax.dot_general(
            sel_s[...], r_d[c], (((0,), (0,)), ((), ())), preferred_element_type=F32
        ).astype(BF)
    llm[mine] = (near + text[mine].astype(F32)).astype(BF)
    outs = [pltpu.make_async_copy(llm.at[mine], llm_out.at[mine], loc_sem.at[0])]
    outs[0].start()
    wait_all(opp, xo_sem.at[0], xo_sem.at[1])
    llm[1 - mine] = (opp[...].astype(F32) + text[1 - mine].astype(F32)).astype(BF)
    outs.append(pltpu.make_async_copy(llm.at[1 - mine], llm_out.at[1 - mine], loc_sem.at[1]))
    outs[1].start()
    block = wfull.at[pl.ds(0, 15 * KB)]
    remote(block, block, ws_sem.at[0], wl_sem.at[0], other).wait_send()
    for cp in got_cps:
        cp.wait()
    for cp in outs:
        cp.wait()


def write_kernel(row_hbm, got_hbm, llm_hbm, out_hbm, grad_hbm, row, got, llm, grad, in_sem, out_sem):
    tiles = D // TILE
    row_cp = pltpu.make_async_copy(row_hbm, row, in_sem.at[tiles])
    row_cp.start()
    ins = []
    for i in range(tiles):
        ins.append(pltpu.make_async_copy(got_hbm.at[:, pl.ds(i * TILE, TILE)], got.at[i], in_sem.at[i]))
        ins[-1].start()
    llm_in = pltpu.make_async_copy(llm_hbm, llm, in_sem.at[tiles + 1])
    llm_in.start()
    row_cp.wait()
    vi = lax.broadcasted_iota(jnp.int32, (VROWS, SLOT), 0)
    place = jnp.where(vi == row[0:1, :], 1.0, 0.0).astype(BF)
    outs = []
    for i in range(tiles):
        ins[i].wait()
        grad[i] = mm(place, got[i]).astype(BF)
        outs.append(pltpu.make_async_copy(grad.at[i], grad_hbm.at[:, pl.ds(i * TILE, TILE)], out_sem.at[i]))
        outs[-1].start()
    llm_in.wait()
    for h in range(NC):
        outs.append(pltpu.make_async_copy(llm.at[h], out_hbm.at[:, pl.ds(h * CW, CW)], out_sem.at[tiles + h]))
        outs[-1].start()
    for cp in outs:
        cp.wait()


def shards(frames, conv_weight, proj_weight, table, audio_pos, token_ids, cotangent):
    relay = relay_matrix()
    consts = [relay, relay.T, channel_matrix(), pack_matrices(), unpack_matrices()]
    consts = [jnp.asarray(m, dtype=BF) for m in consts]
    hbm = pl.BlockSpec(memory_space=pltpu.HBM)
    anywhere = pl.BlockSpec(memory_space=pl.ANY)
    dma = pltpu.SemaphoreType.DMA
    wide = pltpu.VMEM((NC, SLOT, CW), BF)
    llm, got, rows = pl.pallas_call(
        comm_kernel,
        out_shape=[
            jax.ShapeDtypeStruct((NC, SLOT, CW), BF),
            jax.ShapeDtypeStruct((SLOT, D), BF),
            jax.ShapeDtypeStruct((8, SLOT), jnp.int32),
        ],
        in_specs=[hbm] * 12,
        out_specs=[anywhere, anywhere, pl.BlockSpec(memory_space=pltpu.VMEM)],
        scratch_shapes=[
            pltpu.VMEM((1, SLOT), jnp.int32),
            pltpu.VMEM((1, RUN), jnp.int32),
            pltpu.VMEM((FR, CH), BF),
            pltpu.VMEM((TAPS, CH), BF),
            pltpu.VMEM((WROWS, D), BF),
            pltpu.VMEM((SLOT, SLOT), BF),
            pltpu.VMEM((SLOT, SLOT), BF),
            pltpu.VMEM((CH, CH), BF),
            pltpu.VMEM((144, 16), BF),
            pltpu.VMEM((240, 128), BF),
            pltpu.VMEM((SLOT, D), BF),
            pltpu.VMEM((VROWS, D), BF),
            pltpu.VMEM((SLOT, SLOT), BF),
            wide, wide, wide, wide, wide, wide, wide, wide,
            pltpu.VMEM((8, 128), jnp.int32),
            pltpu.VMEM((64, 128), jnp.int32),
            pltpu.VMEM((16, 128), jnp.int32),
            pltpu.VMEM((256, 128), jnp.int32),
            pltpu.VMEM((2, 16, CH), BF),
            pltpu.VMEM((5, FR + 32, 128), F32),
            pltpu.VMEM((5, 32, 128), F32),
            pltpu.VMEM((64, 128), F32),
            pltpu.VMEM((RUN, CH), BF),
            pltpu.VMEM((2, RUN, CH), BF),
            pltpu.VMEM((2, RUN, CH), BF),
            pltpu.VMEM((16, D), F32),
            pltpu.VMEM((16, WP), BF),
            pltpu.VMEM((128, WP), BF),
            pltpu.VMEM((NC, KB, CW), BF),
            pltpu.VMEM((PLANE * KB, CW), BF),
            pltpu.VMEM((2, 2 * SLOT, CH), BF),
            pltpu.VMEM((SLOT, CW), BF),
            pltpu.VMEM((SLOT, CW), BF),
            wide, wide,
            dma((12,)), dma((2,)), dma((2,)), dma((2,)), dma((2,)),
            dma((2, 2)), dma((2, 2)), dma((2, 2)), dma((2, 2)),
            dma((1,)), dma((4,)), dma((4,)), dma((1,)), dma((4,)), dma((4,)), dma((2,)), dma((2,)),
        ],
        compiler_params=pltpu.CompilerParams(
            collective_id=0, has_side_effects=True, vmem_limit_bytes=VMEM_LIMIT
        ),
        name="exchange",
    )(
        token_ids.reshape(1, SLOT), audio_pos.reshape(1, RUN), frames, conv_weight, proj_weight, *consts,
        cotangent, table,
    )
    return pl.pallas_call(
        write_kernel,
        out_shape=[jax.ShapeDtypeStruct((SLOT, D), BF), jax.ShapeDtypeStruct((VROWS, D), BF)],
        in_specs=[hbm] * 3,
        out_specs=[anywhere, anywhere],
        scratch_shapes=[
            pltpu.VMEM((8, SLOT), jnp.int32),
            pltpu.VMEM((D // TILE, SLOT, TILE), BF),
            wide,
            pltpu.VMEM((D // TILE, VROWS, TILE), BF),
            dma((D // TILE + 2,)),
            dma((D // TILE + 2,)),
        ],
        compiler_params=pltpu.CompilerParams(vmem_limit_bytes=VMEM_LIMIT),
        name="write",
    )(rows, got, llm)


def solution(mesh):
    return jax.shard_map(
        shards,
        mesh=mesh,
        in_specs=(
            P("seq", "vocab"),
            P(None, "vocab"),
            P("seq", "vocab"),
            P("seq", "vocab"),
            P("seq"),
            P("seq"),
            P("seq", "vocab"),
        ),
        out_specs=(P("seq", "vocab"), P("seq", "vocab")),
        check_vma=False,
    )
```

```python
import functools

import jax
import jax.numpy as jnp
import numpy as np
from jax import lax
from jax.experimental import pallas as pl
from jax.experimental.pallas import tpu as pltpu
from jax.sharding import PartitionSpec as P

MESH = pl.DeviceIdType.MESH
BF = jnp.bfloat16
F32 = jnp.float32
NX, NZ, NY = 4, 8, 4
N_SEQ = NX * NZ * NY
PLANE = NX * NY
POOL = 4
SLOT = 256
RUN = 128
PART = 32
VROWS = 1188
D = 1792
NC = 2
CW = D // NC
WHOLE = (0, CW)
EARLY = ((0, 384, 0), (384, 512, 1))
CH = 640
FR = 512
TAPS = 31
WROWS = 10
WP = 1152
KB = NZ * WROWS
TILE = 256
VMEM_LIMIT = 60 * 1024 * 1024


def relay_matrix():
    m = np.zeros((SLOT, SLOT), np.float32)
    for z in range(NZ):
        for k in range(2):
            for p in range(PLANE):
                m[p * 16 + k * 8 + z, z * 32 + k * 16 + p] = 1
    return m


def channel_matrix():
    m = np.zeros((CH, CH), np.float32)
    for c in range(CH):
        x, z, y, i = c // 320, (c % 320) // 40, (c % 40) // 10, c % 10
        inner = z * 8 + i if i < 8 else 64 + z * 2 + i - 8
        m[c, (x * 4 + y) * KB + inner] = 1
    return m


def pack_matrices():
    m = np.zeros((9, 16, 16), np.float32)
    for i in range(8):
        m[0, i, i] = 1
        m[1, 8 + i, i] = 1
    for g in range(7):
        for i in range(2):
            m[2 + g, 2 * g + i, 8 + i] = 1
    return m.reshape(9 * 16, 16)


def unpack_matrices():
    top = np.zeros((2, 64, 128), np.float32)
    low = np.zeros((7, 16, 128), np.float32)
    for z in range(NZ):
        for i in range(8):
            top[0, z * 8 + i, z * 16 + i] = 1
            top[1, z * 8 + i, z * 16 + 8 + i] = 1
        for g in range(7):
            for i in range(2):
                low[g, z * 2 + i, z * 16 + 2 * g + i] = 1
    return np.concatenate([top.reshape(128, 128), low.reshape(112, 128)])


def mm(a, b):
    return jnp.dot(a, b, preferred_element_type=F32)


def comm_kernel(
    ids_hbm, pos_hbm, frames_hbm, cw_hbm, w_hbm, relay_hbm, back_hbm, chan_hbm, pack_hbm, unpack_hbm,
    cot_hbm, table_hbm,
    llm_out, got_out, row_ref,
    ids_ref, pos_ref, frames, cw, wown, relay, backm, chan, pack, unpack,
    cot, table, sel_s, f_a, f_b, f_c, f_d, r_a, r_b, r_c, r_d,
    idsnd, idrcv, idcomp, idall, halo, ext, cwf, act, pooled, plo, plp,
    wpadf, wpk, wrz, wst, wfull, xs, far, opp, text, llm, passing,
    loc_sem, halo_sem, idz_sem, idp_sem, wz_sem,
    f1_sem, f2_sem, r1_sem, r2_sem,
    ws_sem, w1_sem, wr_sem, wl_sem, pool_s, pool_r, xx_sem, xo_sem,
):
    s = lax.axis_index("seq")
    v = lax.axis_index("vocab")
    x, z, y = s // 32, (s // 4) % 8, s % 4
    p = x * 4 + y

    def at(xx, zz, yy):
        return ((xx * 8 + zz) * 4 + yy, v)

    def zpeer(d):
        return at(x, lax.rem(z + d, 8), y)

    def ppeer(j):
        return at(lax.rem(x + j // 4, 4), z, lax.rem(y + lax.rem(j, 4), 4))

    def pplace(j):
        return lax.rem(x + j // 4, 4) * 4 + lax.rem(y + lax.rem(j, 4), 4)

    nxt = (lax.rem(s + 1, N_SEQ), v)
    prv = (lax.rem(s + N_SEQ - 1, N_SEQ), v)
    other = (s, 1 - v)
    ahead = (lax.rem((s // 4 + 1) * 4, N_SEQ), v)

    def behind(i):
        return (lax.rem(s + N_SEQ - 4 + i, N_SEQ), v)


    def remote(src, dst, ss, rs, dev):
        return pltpu.make_async_remote_copy(
            src_ref=src, dst_ref=dst, send_sem=ss, recv_sem=rs, device_id=dev, device_id_type=MESH
        )

    def wait_all(block, ss, rs):
        cp = remote(block, block, ss, rs, other)
        cp.wait_send()
        cp.wait_recv()

    def wait_got(block, rs):
        remote(block, block, ws_sem.at[0], rs, other).wait_recv()

    def plane(fn):
        def body(j, c):
            fn(j)
            return c

        lax.fori_loop(1, PLANE, body, 0)

    prow16 = pl.multiple_of(p * 16, 16)
    zrow = pl.multiple_of(z * 32, 32)

    def z_send(src, dst, sem, c, part=WHOLE):
        cols = pl.ds(part[0], part[1])
        for d in (4, 3, 5, 2, 6, 1, 7):
            to = pl.multiple_of(lax.rem(z + d, 8) * 32, 32)
            remote(
                src.at[c, pl.ds(to, 32), cols], dst.at[c, pl.ds(zrow, 32), cols], sem.at[0, c], sem.at[1, c], zpeer(d)
            ).start()
        dst[c, pl.ds(zrow, 32), cols] = src[c, pl.ds(zrow, 32), cols]

    def p_send(src, dst, sem, c, part=WHOLE):
        cols = pl.ds(part[0], part[1])

        def send(j):
            to = pl.multiple_of(pplace(j) * 16, 16)
            remote(
                src.at[c, pl.ds(to, 16), cols], dst.at[c, pl.ds(prow16, 16), cols], sem.at[0, c], sem.at[1, c], ppeer(j)
            ).start()

        plane(send)
        dst[c, pl.ds(prow16, 16), cols] = src[c, pl.ds(prow16, 16), cols]

    def z_wait(dst, sem, c):
        wait_all(dst.at[c, pl.ds(0, 224)], sem.at[0, c], sem.at[1, c])

    def p_wait(dst, sem, c, part=WHOLE):
        wait_all(dst.at[c, pl.ds(0, 240), pl.ds(part[0], part[1])], sem.at[0, c], sem.at[1, c])

    def turn(first, mid, last, sem1, sem2, c, part=WHOLE):
        cols = pl.ds(part[0], part[1])
        p_wait(first, sem1, c, part)
        mid[c, :, cols] = mm(backm[...], first[c, :, cols]).astype(BF)
        z_send(mid, last, sem2, c, part)

    bar = pltpu.get_barrier_semaphore()
    for d in range(1, 8):
        pl.semaphore_signal(bar, inc=1, device_id=zpeer(d), device_id_type=MESH)
    plane(lambda j: pl.semaphore_signal(bar, inc=1, device_id=ppeer(j), device_id_type=MESH))
    for dev in (nxt, prv, other, ahead):
        pl.semaphore_signal(bar, inc=1, device_id=dev, device_id_type=MESH)

    @pl.when(y == 0)
    def _():
        for i in range(4):
            pl.semaphore_signal(bar, inc=1, device_id=behind(i), device_id_type=MESH)


    local = {}
    for i, (name, src, dst) in enumerate(
        (
            ("ids", ids_hbm, ids_ref), ("pos", pos_hbm, pos_ref), ("w", w_hbm, wown), ("pack", pack_hbm, pack),
            ("frames", frames_hbm, frames), ("cot", cot_hbm, cot), ("relay", relay_hbm, relay), ("cw", cw_hbm, cw),
            ("unpack", unpack_hbm, unpack), ("back", back_hbm, backm), ("table", table_hbm, table),
            ("chan", chan_hbm, chan),
        )
    ):
        local[name] = pltpu.make_async_copy(src, dst, loc_sem.at[i])
        local[name].start()

    local["ids"].wait()
    local["pos"].wait()
    bcol = lax.broadcasted_iota(jnp.int32, (SLOT, 1), 0)
    bz, bk, bp = bcol >> 5, (bcol >> 4) & 1, bcol & 15
    low = (((bp >> 2) * 8 + bz) * 4 + (bp & 3)) * VROWS
    rel = ids_ref[...] - low
    qint = lax.broadcasted_iota(jnp.int32, (SLOT, SLOT), 1)
    qi = qint.astype(F32)
    hit = (rel >= 0) & (rel < VROWS)
    first = jnp.min(jnp.where(hit, qi, 4096.0), axis=1, keepdims=True)
    last = jnp.max(jnp.where(hit, qi, -1.0), axis=1, keepdims=True)
    chosen = jnp.where(bk == 0, first, jnp.where(last > first, last, -1.0))
    picked = qi == chosen
    sel_s[...] = jnp.where(picked, 1.0, 0.0).astype(BF)
    code = jnp.sum(jnp.where(picked, (qint * 2048 + rel + 1).astype(F32), 0.0), axis=1, keepdims=True)
    brow = lax.broadcasted_iota(jnp.int32, (SLOT, SLOT), 0)
    diag = brow == qint
    coderow = jnp.sum(jnp.where(diag, code, 0.0), axis=0, keepdims=True).astype(jnp.int32)
    start = pos_ref[0:1, 0:1]
    eight = lax.broadcasted_iota(jnp.int32, (8, 128), 0)
    idsnd[...] = jnp.where(
        eight == 0, coderow[:, 0:128], jnp.where(eight == 1, coderow[:, 128:256], jnp.broadcast_to(start, (8, 128)))
    )
    zrow8 = pl.multiple_of(z * 8, 8)
    idrcv[pl.ds(zrow8, 8), :] = idsnd[...]

    local["w"].wait()
    local["pack"].wait()
    wpadf[...] = jnp.zeros_like(wpadf)
    wpadf[0:WROWS, :] = wown[...].astype(F32)
    wp = wpadf[...].astype(BF)
    half = D // 2
    wpk[:, 0:half] = (mm(pack[0:16], wp[:, 0:half]) + mm(pack[16:32], wp[:, half:])).astype(BF)
    tail = jnp.zeros((16, 256), F32)
    for g in range(7):
        tail = tail + mm(pack[32 + 16 * g : 48 + 16 * g], wp[:, 256 * g : 256 * g + 256])
    wpk[:, half:] = tail.astype(BF)
    zrow16 = pl.multiple_of(z * 16, 16)
    wrz[pl.ds(zrow16, 16), :] = wpk[...]

    local["cot"].wait()
    local["relay"].wait()

    def bucketed(c):
        f_a[c] = mm(relay[...], mm(sel_s[...], cot[:, c * CW : (c + 1) * CW]).astype(BF)).astype(BF)

    bucketed(0)
    local["frames"].wait()

    @pl.when(y == 0)
    def _():
        pl.semaphore_wait(bar, 7 + PLANE - 1 + 8)

    @pl.when(y > 0)
    def _():
        pl.semaphore_wait(bar, 7 + PLANE - 1 + 4)


    for d in (1, 7, 2, 6, 3, 5, 4):
        remote(idsnd, idrcv.at[pl.ds(zrow8, 8)], idz_sem.at[0], idz_sem.at[1], zpeer(d)).start()
    remote(frames.at[pl.ds(FR - 16, 16)], halo.at[0], halo_sem.at[0], halo_sem.at[1], nxt).start()
    remote(frames.at[pl.ds(0, 16)], halo.at[1], halo_sem.at[0], halo_sem.at[1], prv).start()
    def ring_block(k):
        return wrz.at[pl.ds(pl.multiple_of(lax.rem(z + k, 8) * 16, 16), 16)]

    for d in (2, 6, 1, 7):
        remote(wpk, ring_block(0), wz_sem.at[0], wz_sem.at[1 if d in (1, 7) else d], zpeer(d)).start()
    for part in EARLY:
        p_send(f_a, f_b, f1_sem.at[part[2]], 0, part)
    bucketed(1)
    for name in ("cw", "unpack", "back", "table", "chan"):
        local[name].wait()

    wait_all(idrcv.at[pl.ds(0, 56)], idz_sem.at[0], idz_sem.at[1])
    even = idrcv[pl.ds(0, 8, stride=8), :]
    odd = idrcv[pl.ds(1, 8, stride=8), :]
    lane8 = lax.broadcasted_iota(jnp.int32, (8, 128), 1)
    at_start = lax.rem(z + 1, 4) * 32
    idcomp[...] = jnp.where(lane8 == at_start, idrcv[pl.ds(2, 8, stride=8), :], jnp.where(z < 4, even, odd))
    prow8 = pl.multiple_of(p * 8, 8)
    idall[pl.ds(prow8, 8), :] = idcomp[...]
    plane(
        lambda j: remote(idcomp, idall.at[pl.ds(prow8, 8)], idp_sem.at[0], idp_sem.at[1], ppeer(j)).start()
    )
    p_send(f_a, f_b, f1_sem.at[0], 1)

    wait_got(ring_block(6), wz_sem.at[2])
    remote(ring_block(6), ring_block(6), wz_sem.at[0], wz_sem.at[1], zpeer(1)).start()
    remote(ring_block(6), ring_block(6), wz_sem.at[0], wz_sem.at[1], zpeer(2)).start()
    wait_got(ring_block(2), wz_sem.at[6])
    remote(ring_block(2), ring_block(2), wz_sem.at[0], wz_sem.at[1], zpeer(7)).start()
    wait_all(halo, halo_sem.at[0], halo_sem.at[1])
    for l in range(5):
        cols = slice(128 * l, 128 * l + 128)
        ext[l, 16 : 16 + FR, :] = frames[:, cols].astype(F32)
        ext[l, 0:16, :] = jnp.where(s > 0, halo[0, :, cols].astype(F32), 0.0)
        ext[l, 16 + FR : 32 + FR, :] = jnp.where(s < N_SEQ - 1, halo[1, :, cols].astype(F32), 0.0)
        cwf[l, 0:TAPS, :] = cw[:, cols].astype(F32)

    def conv(i, carry):
        l, rb = i // 8, lax.rem(i, 8)
        r0 = pl.multiple_of(rb * 64, 64)
        acc = jnp.zeros((64, 128), F32)
        for j in range(TAPS):
            acc = acc + ext[l, pl.ds(r0 + (j + 1), 64), :] * cwf[l, pl.ds(j, 1), :]
        act[...] = ext[l, pl.ds(r0 + 16, 64), :] + acc / (1.0 + jnp.exp(-acc))
        total = act[pl.ds(0, 16, stride=4), :]
        for k in range(1, POOL):
            total = total + act[pl.ds(k, 16, stride=4), :]
        pooled[pl.ds(pl.multiple_of(rb * 16, 16), 16), pl.ds(pl.multiple_of(l * 128, 128), 128)] = (
            total * (1.0 / POOL)
        ).astype(BF)
        return carry

    lax.fori_loop(0, 20, conv, 0)

    for part in EARLY:
        turn(f_b, f_c, f_d, f1_sem.at[part[2]], f2_sem, 0, part)
    lax.fori_loop(20, 40, conv, 0)
    plo[v] = mm(pooled[...], chan[...]).astype(BF)
    core_cp = remote(plo.at[v], plo.at[v], pool_s.at[0], pool_r.at[0], other)
    next_cp = remote(plo.at[v], plp.at[v], pool_s.at[1], pool_r.at[1], nxt)
    core_cp.start()

    @pl.when(y < 3)
    def _():
        next_cp.start()

    @pl.when(y == 3)
    def _():
        last = pl.ds(3 * PART, PART)
        remote(plo.at[v, last], plp.at[v, last], pool_s.at[1], pool_r.at[1], ahead).start()
        for i in range(3):
            remote(plo.at[v, pl.ds(i * PART, PART)], passing, pool_s.at[1], pool_r.at[4], at(x, z, i)).start()


    wait_got(wrz.at[pl.ds(0, 80)], wz_sem.at[1])
    sent = wrz.at[pl.ds(0, 112)]
    remote(sent, sent, wz_sem.at[0], wz_sem.at[1], other).wait_send()
    prow80 = pl.multiple_of(p * KB, 16)
    packed = wrz[...]
    for c in range(NC):
        wst[c, 0:64, :] = mm(unpack[64 * c : 64 * c + 64], packed[:, 0:half]).astype(BF)
    for g in range(7):
        piece = mm(unpack[128 + 16 * g : 144 + 16 * g], packed[:, half:]).astype(BF)
        for b in range(2):
            col = 256 * g + 128 * b
            c, off = col // CW, col % CW
            wst[c, 64:KB, off : off + 128] = piece[:, 128 * b : 128 * b + 128]
    mine = lax.rem(x, 2)
    wfull[pl.ds(prow80, KB), :] = wst[mine]

    def wblock(f, g):
        return wfull.at[pl.ds(pl.multiple_of((lax.rem(x + f, 4) * 4 + lax.rem(y + g, 4)) * KB, 16), KB)]

    def wsend(block, dst, sem, dev):
        remote(block, dst, ws_sem.at[0], sem, dev).start()

    def wsecond(f):
        up, down = (wr_sem.at[f], wl_sem.at[0]) if f < 2 else (wl_sem.at[0], wr_sem.at[f])
        wsend(wblock(f, 0), wblock(f, 0), up, at(x, z, lax.rem(y + 1, 4)))
        wsend(wblock(f, 0), wblock(f, 0), down, at(x, z, lax.rem(y + 3, 4)))

    def w2relay(f):
        near, to = (3, 1) if f < 2 else (1, 3)
        wait_got(wblock(f, near), wr_sem.at[f])
        wsend(wblock(f, near), wblock(f, near), wl_sem.at[0], at(x, z, lax.rem(y + to, 4)))

    def xpeer(f):
        return at(lax.rem(x + f, 4), z, y)

    for f in (1, 3, 2):
        wsend(wst.at[mine if f == 2 else 1 - mine], wblock(0, 0), w1_sem.at[f], xpeer(f))
    wsecond(0)

    wait_all(idall.at[pl.ds(0, 120)], idp_sem.at[0], idp_sem.at[1])
    dup = []
    for i in range(PLANE):
        piece = idall[8 * i : 8 * i + 8, :]
        dup += [piece, piece]
    every = jnp.concatenate(dup, axis=0)
    lane = lax.broadcasted_iota(jnp.int32, (SLOT, 128), 1)
    rrow = lax.broadcasted_iota(jnp.int32, (SLOT, 128), 0)
    want = lax.rem(z, 4) * 32 + ((rrow >> 3) & 1) * 16 + p
    codes = jnp.sum(jnp.where(lane == want, every, 0).astype(F32), axis=1, keepdims=True).astype(jnp.int32)
    starts = jnp.sum(jnp.where(lane == at_start, every, 0).astype(F32), axis=1, keepdims=True).astype(jnp.int32)
    mrow = lax.broadcasted_iota(jnp.int32, (128, 128), 0)
    mcol = lax.broadcasted_iota(jnp.int32, (128, 128), 1)
    stcol = jnp.sum(jnp.where(mcol == at_start, idall[...], 0).astype(F32), axis=1, keepdims=True)
    strow = jnp.sum(jnp.where(mrow == mcol, stcol, 0.0), axis=0, keepdims=True)
    rcol = lax.broadcasted_iota(jnp.int32, (SLOT, 1), 0)
    rp = rcol >> 4
    rs = ((rp >> 2) * 8 + (rcol & 7)) * 4 + (rp & 3)
    rprev = rs - 1
    prevm = jnp.where(rs == 0, -1, ((rprev >> 5) * 4 + (rprev & 3)) * 8 + ((rprev >> 2) & 7))
    prevst = jnp.sum(jnp.where(lane == prevm, strow, 0.0), axis=1, keepdims=True).astype(jnp.int32)
    prevst = jnp.where(rs == 0, -4096, prevst)
    rslot = rs * SLOT + (codes >> 11)
    audio = ((rslot >= starts) & (rslot < starts + RUN)) | ((rslot >= prevst) & (rslot < prevst + RUN))
    rowid = jnp.where(audio | (codes == 0), -1, (codes & 2047) - 1)
    vi = lax.broadcasted_iota(jnp.int32, (SLOT, VROWS), 1)
    look = jnp.where(vi == rowid, 1.0, 0.0).astype(BF)

    r_a[0] = mm(look, table[:, 0:CW]).astype(BF)
    p_send(r_a, r_b, r1_sem, 0)
    r_a[1] = mm(look, table[:, CW:]).astype(BF)

    rowrow = jnp.sum(jnp.where(diag, rowid.astype(F32), 0.0), axis=0, keepdims=True).astype(jnp.int32)
    sprev = lax.rem(s + N_SEQ - 1, N_SEQ)
    mprev = ((sprev // 32) * 4 + lax.rem(sprev, 4)) * 8 + lax.rem(sprev // 4, 8)
    mlane = lax.broadcasted_iota(jnp.int32, (1, 128), 1)
    before = jnp.sum(jnp.where(mlane == mprev, strow, 0.0), axis=1, keepdims=True).astype(jnp.int32)
    before = jnp.where(s > 0, before, -4096)

    p_send(r_a, r_b, r1_sem, 1)
    @pl.when(y < 3)
    def _():
        part = pl.ds(pl.multiple_of(y * PART, PART), PART)
        wait_got(passing, pool_r.at[4])
        remote(passing, plp.at[v, part], pool_s.at[4], pool_r.at[1], ahead).start()

    turn(f_b, f_c, f_d, f1_sem.at[0], f2_sem, 1)
    for f in (1, 3, 2):
        wait_got(wblock(f, 0), w1_sem.at[4 - f])
        wsecond(f)

    turn(r_b, r_c, r_d, r1_sem, r2_sem, 0)
    next_cp.wait()
    fwd_cp = remote(plp.at[v], plp.at[v], pool_s.at[2], pool_r.at[2], other)
    fwd_cp.start()
    w2relay(0)

    core_cp.wait()
    fwd_cp.wait()
    def xsend(src, dst, sem, f):
        remote(src, dst, sem.at[0], sem.at[1], xpeer(f)).start()

    qslot = s * SLOT + lax.broadcasted_iota(jnp.int32, (SLOT, RUN), 0)
    prun = lax.broadcasted_iota(jnp.int32, (SLOT, RUN), 1)
    own_sel = jnp.where(qslot == start + prun, 1.0, 0.0).astype(BF)
    prev_sel = jnp.where(qslot == before + prun, 1.0, 0.0).astype(BF)
    for h in range(2):
        xs[h, 0:SLOT, :] = (mm(own_sel, plo[h]) + mm(prev_sel, plp[h])).astype(BF)
    xsend(xs.at[v, pl.ds(0, RUN)], xs.at[v, pl.ds(SLOT, RUN)], xx_sem, 1)
    xsend(xs.at[v, pl.ds(RUN, RUN)], xs.at[v, pl.ds(SLOT + RUN, RUN)], xx_sem, 3)

    turn(r_b, r_c, r_d, r1_sem, r2_sem, 1)
    for f in (1, 3, 2):
        w2relay(f)

    wait_all(xs.at[v, pl.ds(SLOT, SLOT)], xx_sem.at[0], xx_sem.at[1])
    x_cp = remote(xs.at[v, pl.ds(SLOT, SLOT)], xs.at[v, pl.ds(SLOT, SLOT)], pool_s.at[3], pool_r.at[3], other)
    x_cp.start()

    for c in range(NC):
        z_wait(f_d, f2_sem, c)
    got_cps = []
    for c in range(NC):
        f_c[c] = mm(relay[...], f_d[c]).astype(BF)
        got_cps.append(pltpu.make_async_copy(f_c.at[c], got_out.at[:, pl.ds(c * CW, CW)], loc_sem.at[2 + c]))
        got_cps[-1].start()
    row_ref[...] = jnp.broadcast_to(rowrow, (8, SLOT))
    x_cp.wait()
    wait_got(wfull.at[pl.ds(0, 8 * KB)], wl_sem.at[0])
    far[...] = (mm(xs[0, SLOT:, :], wfull[0:CH, :]) + mm(xs[1, SLOT:, :], wfull[CH:, :])).astype(BF)
    xsend(far.at[pl.ds(0, RUN)], opp.at[pl.ds(0, RUN)], xo_sem, 3)
    xsend(far.at[pl.ds(RUN, RUN)], opp.at[pl.ds(RUN, RUN)], xo_sem, 1)
    near = mm(xs[0, 0:SLOT, :], wfull[0:CH, :]) + mm(xs[1, 0:SLOT, :], wfull[CH:, :])
    near = near.astype(BF).astype(F32)
    for c in range(NC):
        z_wait(r_d, r2_sem, c)
        text[c] = lax.dot_general(
            sel_s[...], r_d[c], (((0,), (0,)), ((), ())), preferred_element_type=F32
        ).astype(BF)
    llm[mine] = (near + text[mine].astype(F32)).astype(BF)
    outs = [pltpu.make_async_copy(llm.at[mine], llm_out.at[mine], loc_sem.at[0])]
    outs[0].start()
    wait_all(opp, xo_sem.at[0], xo_sem.at[1])
    llm[1 - mine] = (opp[...].astype(F32) + text[1 - mine].astype(F32)).astype(BF)
    outs.append(pltpu.make_async_copy(llm.at[1 - mine], llm_out.at[1 - mine], loc_sem.at[1]))
    outs[1].start()
    @pl.when(y < 3)
    def _():
        remote(passing, passing, pool_s.at[4], pool_r.at[4], other).wait_send()

    block = wfull.at[pl.ds(0, 15 * KB)]
    remote(block, block, ws_sem.at[0], wl_sem.at[0], other).wait_send()
    for cp in got_cps:
        cp.wait()
    for cp in outs:
        cp.wait()


def write_kernel(row_hbm, got_hbm, llm_hbm, out_hbm, grad_hbm, row, got, llm, grad, place, in_sem, out_sem):
    tiles = D // TILE

    def get(i):
        cols = pl.ds(pl.multiple_of(i * TILE, TILE), TILE)
        return pltpu.make_async_copy(got_hbm.at[:, cols], got.at[i], in_sem.at[i])

    def put(i):
        cols = pl.ds(pl.multiple_of(i * TILE, TILE), TILE)
        return pltpu.make_async_copy(grad.at[i], grad_hbm.at[:, cols], out_sem.at[i])

    def put_llm(h):
        return pltpu.make_async_copy(llm.at[h], out_hbm.at[:, pl.ds(h * CW, CW)], out_sem.at[tiles + h])

    row_cp = pltpu.make_async_copy(row_hbm, row, in_sem.at[tiles])
    row_cp.start()
    llm_in = pltpu.make_async_copy(llm_hbm, llm, in_sem.at[tiles + 1])
    for i in range(tiles):
        get(i).start()
    llm_in.start()
    row_cp.wait()
    vi = lax.broadcasted_iota(jnp.int32, (VROWS, SLOT), 0)
    place[...] = jnp.where(vi == row[0:1, :], 1.0, 0.0).astype(BF)

    def tile(i, c):
        get(i).wait()
        grad[i] = mm(place[...], got[i]).astype(BF)
        put(i).start()
        return c

    lax.fori_loop(0, tiles, tile, 0)
    llm_in.wait()
    for h in range(NC):
        put_llm(h).start()
    for i in range(tiles):
        put(i).wait()
    for h in range(NC):
        put_llm(h).wait()


def shards(frames, conv_weight, proj_weight, table, audio_pos, token_ids, cotangent):
    relay = relay_matrix()
    consts = [relay, relay.T, channel_matrix(), pack_matrices(), unpack_matrices()]
    consts = [jnp.asarray(m, dtype=BF) for m in consts]
    hbm = pl.BlockSpec(memory_space=pltpu.HBM)
    anywhere = pl.BlockSpec(memory_space=pl.ANY)
    dma = pltpu.SemaphoreType.DMA
    wide = pltpu.VMEM((NC, SLOT, CW), BF)
    llm, got, rows = pl.pallas_call(
        comm_kernel,
        out_shape=[
            jax.ShapeDtypeStruct((NC, SLOT, CW), BF),
            jax.ShapeDtypeStruct((SLOT, D), BF),
            jax.ShapeDtypeStruct((8, SLOT), jnp.int32),
        ],
        in_specs=[hbm] * 12,
        out_specs=[anywhere, anywhere, pl.BlockSpec(memory_space=pltpu.VMEM)],
        scratch_shapes=[
            pltpu.VMEM((1, SLOT), jnp.int32),
            pltpu.VMEM((1, RUN), jnp.int32),
            pltpu.VMEM((FR, CH), BF),
            pltpu.VMEM((TAPS, CH), BF),
            pltpu.VMEM((WROWS, D), BF),
            pltpu.VMEM((SLOT, SLOT), BF),
            pltpu.VMEM((SLOT, SLOT), BF),
            pltpu.VMEM((CH, CH), BF),
            pltpu.VMEM((144, 16), BF),
            pltpu.VMEM((240, 128), BF),
            pltpu.VMEM((SLOT, D), BF),
            pltpu.VMEM((VROWS, D), BF),
            pltpu.VMEM((SLOT, SLOT), BF),
            wide, wide, wide, wide, wide, wide, wide, wide,
            pltpu.VMEM((8, 128), jnp.int32),
            pltpu.VMEM((64, 128), jnp.int32),
            pltpu.VMEM((8, 128), jnp.int32),
            pltpu.VMEM((128, 128), jnp.int32),
            pltpu.VMEM((2, 16, CH), BF),
            pltpu.VMEM((5, FR + 32, 128), F32),
            pltpu.VMEM((5, 32, 128), F32),
            pltpu.VMEM((64, 128), F32),
            pltpu.VMEM((RUN, CH), BF),
            pltpu.VMEM((2, RUN, CH), BF),
            pltpu.VMEM((2, RUN, CH), BF),
            pltpu.VMEM((16, D), F32),
            pltpu.VMEM((16, WP), BF),
            pltpu.VMEM((128, WP), BF),
            pltpu.VMEM((NC, KB, CW), BF),
            pltpu.VMEM((PLANE * KB, CW), BF),
            pltpu.VMEM((2, 2 * SLOT, CH), BF),
            pltpu.VMEM((SLOT, CW), BF),
            pltpu.VMEM((SLOT, CW), BF),
            wide, wide,
            pltpu.VMEM((PART, CH), BF),
            dma((12,)), dma((2,)), dma((2,)), dma((2,)), dma((7,)),
            dma((2, 2, 2)), dma((2, 2)), dma((2, 2)), dma((2, 2)),
            dma((1,)), dma((4,)), dma((4,)), dma((1,)), dma((5,)), dma((5,)), dma((2,)), dma((2,)),
        ],
        compiler_params=pltpu.CompilerParams(
            collective_id=0, has_side_effects=True, vmem_limit_bytes=VMEM_LIMIT
        ),
        name="exchange",
    )(
        token_ids.reshape(1, SLOT), audio_pos.reshape(1, RUN), frames, conv_weight, proj_weight, *consts,
        cotangent, table,
    )
    return pl.pallas_call(
        write_kernel,
        out_shape=[jax.ShapeDtypeStruct((SLOT, D), BF), jax.ShapeDtypeStruct((VROWS, D), BF)],
        in_specs=[hbm] * 3,
        out_specs=[anywhere, anywhere],
        scratch_shapes=[
            pltpu.VMEM((8, SLOT), jnp.int32),
            pltpu.VMEM((D // TILE, SLOT, TILE), BF),
            wide,
            pltpu.VMEM((D // TILE, VROWS, TILE), BF),
            pltpu.VMEM((VROWS, SLOT), BF),
            dma((D // TILE + 2,)),
            dma((D // TILE + 2,)),
        ],
        compiler_params=pltpu.CompilerParams(vmem_limit_bytes=VMEM_LIMIT),
        name="write",
    )(rows, got, llm)


def solution(mesh):
    return jax.shard_map(
        shards,
        mesh=mesh,
        in_specs=(
            P("seq", "vocab"),
            P(None, "vocab"),
            P("seq", "vocab"),
            P("seq", "vocab"),
            P("seq"),
            P("seq"),
            P("seq", "vocab"),
        ),
        out_specs=(P("seq", "vocab"), P("seq", "vocab")),
        check_vma=False,
    )
```

```python
import functools

import jax
import jax.numpy as jnp
import numpy as np
from jax import lax
from jax.experimental import pallas as pl
from jax.experimental.pallas import tpu as pltpu
from jax.sharding import PartitionSpec as P

MESH = pl.DeviceIdType.MESH
BF = jnp.bfloat16
F32 = jnp.float32
NX, NZ, NY = 4, 8, 4
N_SEQ = NX * NZ * NY
PLANE = NX * NY
POOL = 4
SLOT = 256
RUN = 128
PART = 32
VROWS = 1188
D = 1792
NC = 2
CW = D // NC
WHOLE = (0, CW)
EARLY = ((0, 384, 0), (384, 512, 1))
CH = 640
FR = 512
TAPS = 31
WROWS = 10
WP = 1152
KB = NZ * WROWS
TILE = 256
PRE = 3
VMEM_LIMIT = 60 * 1024 * 1024


def relay_matrix():
    m = np.zeros((SLOT, SLOT), np.float32)
    for z in range(NZ):
        for k in range(2):
            for p in range(PLANE):
                m[p * 16 + k * 8 + z, z * 32 + k * 16 + p] = 1
    return m


def channel_matrix():
    m = np.zeros((CH, CH), np.float32)
    for c in range(CH):
        x, z, y, i = c // 320, (c % 320) // 40, (c % 40) // 10, c % 10
        inner = z * 8 + i if i < 8 else 64 + z * 2 + i - 8
        m[c, (x * 4 + y) * KB + inner] = 1
    return m


def pack_matrices():
    m = np.zeros((9, 16, 16), np.float32)
    for i in range(8):
        m[0, i, i] = 1
        m[1, 8 + i, i] = 1
    for g in range(7):
        for i in range(2):
            m[2 + g, 2 * g + i, 8 + i] = 1
    return m.reshape(9 * 16, 16)


def unpack_matrices():
    top = np.zeros((2, 64, 128), np.float32)
    low = np.zeros((7, 16, 128), np.float32)
    for z in range(NZ):
        for i in range(8):
            top[0, z * 8 + i, z * 16 + i] = 1
            top[1, z * 8 + i, z * 16 + 8 + i] = 1
        for g in range(7):
            for i in range(2):
                low[g, z * 2 + i, z * 16 + 2 * g + i] = 1
    return np.concatenate([top.reshape(128, 128), low.reshape(112, 128)])


def mm(a, b):
    return jnp.dot(a, b, preferred_element_type=F32)


def comm_kernel(
    ids_hbm, pos_hbm, frames_hbm, cw_hbm, w_hbm, relay_hbm, back_hbm, chan_hbm, pack_hbm, unpack_hbm,
    cot_hbm, table_hbm,
    llm_out, got_out, gpre_out, row_ref,
    ids_ref, pos_ref, frames, cw, wown, relay, backm, chan, pack, unpack,
    cot, table, sel_s, f_a, f_b, f_c, f_d, r_a, r_b, r_c, r_d,
    idsnd, idrcv, idcomp, idall, halo, ext, cwf, act, pooled, plo, plp,
    wpadf, wpk, wrz, wst, wfull, xs, far, opp, text, llm, passing, place, gpre,
    loc_sem, halo_sem, idz_sem, idp_sem, wz_sem,
    f1_sem, f2_sem, r1_sem, r2_sem,
    ws_sem, w1_sem, wr_sem, wl_sem, pool_s, pool_r, xx_sem, xo_sem,
):
    s = lax.axis_index("seq")
    v = lax.axis_index("vocab")
    x, z, y = s // 32, (s // 4) % 8, s % 4
    p = x * 4 + y

    def at(xx, zz, yy):
        return ((xx * 8 + zz) * 4 + yy, v)

    def zpeer(d):
        return at(x, lax.rem(z + d, 8), y)

    def ppeer(j):
        return at(lax.rem(x + j // 4, 4), z, lax.rem(y + lax.rem(j, 4), 4))

    def pplace(j):
        return lax.rem(x + j // 4, 4) * 4 + lax.rem(y + lax.rem(j, 4), 4)

    nxt = (lax.rem(s + 1, N_SEQ), v)
    prv = (lax.rem(s + N_SEQ - 1, N_SEQ), v)
    other = (s, 1 - v)
    ahead = (lax.rem((s // 4 + 1) * 4, N_SEQ), v)

    def behind(i):
        return (lax.rem(s + N_SEQ - 4 + i, N_SEQ), v)


    def remote(src, dst, ss, rs, dev):
        return pltpu.make_async_remote_copy(
            src_ref=src, dst_ref=dst, send_sem=ss, recv_sem=rs, device_id=dev, device_id_type=MESH
        )

    def wait_all(block, ss, rs):
        cp = remote(block, block, ss, rs, other)
        cp.wait_send()
        cp.wait_recv()

    def wait_got(block, rs):
        remote(block, block, ws_sem.at[0], rs, other).wait_recv()

    def plane(fn):
        def body(j, c):
            fn(j)
            return c

        lax.fori_loop(1, PLANE, body, 0)

    prow16 = pl.multiple_of(p * 16, 16)
    zrow = pl.multiple_of(z * 32, 32)

    def z_send(src, dst, sem, c, part=WHOLE):
        cols = pl.ds(part[0], part[1])
        for d in (4, 3, 5, 2, 6, 1, 7):
            to = pl.multiple_of(lax.rem(z + d, 8) * 32, 32)
            remote(
                src.at[c, pl.ds(to, 32), cols], dst.at[c, pl.ds(zrow, 32), cols], sem.at[0, c], sem.at[1, c], zpeer(d)
            ).start()
        dst[c, pl.ds(zrow, 32), cols] = src[c, pl.ds(zrow, 32), cols]

    def p_send(src, dst, sem, c, part=WHOLE):
        cols = pl.ds(part[0], part[1])

        def send(j):
            to = pl.multiple_of(pplace(j) * 16, 16)
            remote(
                src.at[c, pl.ds(to, 16), cols], dst.at[c, pl.ds(prow16, 16), cols], sem.at[0, c], sem.at[1, c], ppeer(j)
            ).start()

        plane(send)
        dst[c, pl.ds(prow16, 16), cols] = src[c, pl.ds(prow16, 16), cols]

    def z_wait(dst, sem, c):
        wait_all(dst.at[c, pl.ds(0, 224)], sem.at[0, c], sem.at[1, c])

    def p_wait(dst, sem, c, part=WHOLE):
        wait_all(dst.at[c, pl.ds(0, 240), pl.ds(part[0], part[1])], sem.at[0, c], sem.at[1, c])

    def turn(first, mid, last, sem1, sem2, c, part=WHOLE):
        cols = pl.ds(part[0], part[1])
        p_wait(first, sem1, c, part)
        mid[c, :, cols] = mm(backm[...], first[c, :, cols]).astype(BF)
        z_send(mid, last, sem2, c, part)

    bar = pltpu.get_barrier_semaphore()
    for d in range(1, 8):
        pl.semaphore_signal(bar, inc=1, device_id=zpeer(d), device_id_type=MESH)
    plane(lambda j: pl.semaphore_signal(bar, inc=1, device_id=ppeer(j), device_id_type=MESH))
    for dev in (nxt, prv, other, ahead):
        pl.semaphore_signal(bar, inc=1, device_id=dev, device_id_type=MESH)

    @pl.when(y == 0)
    def _():
        for i in range(4):
            pl.semaphore_signal(bar, inc=1, device_id=behind(i), device_id_type=MESH)


    local = {}
    for i, (name, src, dst) in enumerate(
        (
            ("ids", ids_hbm, ids_ref), ("pos", pos_hbm, pos_ref), ("w", w_hbm, wown), ("pack", pack_hbm, pack),
            ("frames", frames_hbm, frames), ("cot", cot_hbm, cot), ("relay", relay_hbm, relay), ("cw", cw_hbm, cw),
            ("unpack", unpack_hbm, unpack), ("back", back_hbm, backm), ("table", table_hbm, table),
            ("chan", chan_hbm, chan),
        )
    ):
        local[name] = pltpu.make_async_copy(src, dst, loc_sem.at[i])
        local[name].start()

    local["ids"].wait()
    local["pos"].wait()
    bcol = lax.broadcasted_iota(jnp.int32, (SLOT, 1), 0)
    bz, bk, bp = bcol >> 5, (bcol >> 4) & 1, bcol & 15
    low = (((bp >> 2) * 8 + bz) * 4 + (bp & 3)) * VROWS
    rel = ids_ref[...] - low
    qint = lax.broadcasted_iota(jnp.int32, (SLOT, SLOT), 1)
    qi = qint.astype(F32)
    hit = (rel >= 0) & (rel < VROWS)
    first = jnp.min(jnp.where(hit, qi, 4096.0), axis=1, keepdims=True)
    last = jnp.max(jnp.where(hit, qi, -1.0), axis=1, keepdims=True)
    chosen = jnp.where(bk == 0, first, jnp.where(last > first, last, -1.0))
    picked = qi == chosen
    sel_s[...] = jnp.where(picked, 1.0, 0.0).astype(BF)
    code = jnp.sum(jnp.where(picked, (qint * 2048 + rel + 1).astype(F32), 0.0), axis=1, keepdims=True)
    brow = lax.broadcasted_iota(jnp.int32, (SLOT, SLOT), 0)
    diag = brow == qint
    coderow = jnp.sum(jnp.where(diag, code, 0.0), axis=0, keepdims=True).astype(jnp.int32)
    start = pos_ref[0:1, 0:1]
    eight = lax.broadcasted_iota(jnp.int32, (8, 128), 0)
    idsnd[...] = jnp.where(
        eight == 0, coderow[:, 0:128], jnp.where(eight == 1, coderow[:, 128:256], jnp.broadcast_to(start, (8, 128)))
    )
    zrow8 = pl.multiple_of(z * 8, 8)
    idrcv[pl.ds(zrow8, 8), :] = idsnd[...]

    local["w"].wait()
    local["pack"].wait()
    wpadf[...] = jnp.zeros_like(wpadf)
    wpadf[0:WROWS, :] = wown[...].astype(F32)
    wp = wpadf[...].astype(BF)
    half = D // 2
    wpk[:, 0:half] = (mm(pack[0:16], wp[:, 0:half]) + mm(pack[16:32], wp[:, half:])).astype(BF)
    tail = jnp.zeros((16, 256), F32)
    for g in range(7):
        tail = tail + mm(pack[32 + 16 * g : 48 + 16 * g], wp[:, 256 * g : 256 * g + 256])
    wpk[:, half:] = tail.astype(BF)
    zrow16 = pl.multiple_of(z * 16, 16)
    wrz[pl.ds(zrow16, 16), :] = wpk[...]

    local["cot"].wait()
    local["relay"].wait()

    def bucketed(c):
        f_a[c] = mm(relay[...], mm(sel_s[...], cot[:, c * CW : (c + 1) * CW]).astype(BF)).astype(BF)

    bucketed(0)
    local["frames"].wait()

    @pl.when(y == 0)
    def _():
        pl.semaphore_wait(bar, 7 + PLANE - 1 + 8)

    @pl.when(y > 0)
    def _():
        pl.semaphore_wait(bar, 7 + PLANE - 1 + 4)


    for d in (1, 7, 2, 6, 3, 5, 4):
        remote(idsnd, idrcv.at[pl.ds(zrow8, 8)], idz_sem.at[0], idz_sem.at[1], zpeer(d)).start()
    remote(frames.at[pl.ds(FR - 16, 16)], halo.at[0], halo_sem.at[0], halo_sem.at[1], nxt).start()
    remote(frames.at[pl.ds(0, 16)], halo.at[1], halo_sem.at[0], halo_sem.at[1], prv).start()
    def ring_block(k):
        return wrz.at[pl.ds(pl.multiple_of(lax.rem(z + k, 8) * 16, 16), 16)]

    for d in (2, 6, 1, 7):
        remote(wpk, ring_block(0), wz_sem.at[0], wz_sem.at[1 if d in (1, 7) else d], zpeer(d)).start()
    for part in EARLY:
        p_send(f_a, f_b, f1_sem.at[part[2]], 0, part)
    bucketed(1)
    for name in ("cw", "unpack", "back", "table", "chan"):
        local[name].wait()

    wait_all(idrcv.at[pl.ds(0, 56)], idz_sem.at[0], idz_sem.at[1])
    even = idrcv[pl.ds(0, 8, stride=8), :]
    odd = idrcv[pl.ds(1, 8, stride=8), :]
    lane8 = lax.broadcasted_iota(jnp.int32, (8, 128), 1)
    at_start = lax.rem(z + 1, 4) * 32
    idcomp[...] = jnp.where(lane8 == at_start, idrcv[pl.ds(2, 8, stride=8), :], jnp.where(z < 4, even, odd))
    prow8 = pl.multiple_of(p * 8, 8)
    idall[pl.ds(prow8, 8), :] = idcomp[...]
    plane(
        lambda j: remote(idcomp, idall.at[pl.ds(prow8, 8)], idp_sem.at[0], idp_sem.at[1], ppeer(j)).start()
    )
    p_send(f_a, f_b, f1_sem.at[0], 1)

    wait_got(ring_block(6), wz_sem.at[2])
    remote(ring_block(6), ring_block(6), wz_sem.at[0], wz_sem.at[1], zpeer(1)).start()
    remote(ring_block(6), ring_block(6), wz_sem.at[0], wz_sem.at[1], zpeer(2)).start()
    wait_got(ring_block(2), wz_sem.at[6])
    remote(ring_block(2), ring_block(2), wz_sem.at[0], wz_sem.at[1], zpeer(7)).start()
    wait_all(halo, halo_sem.at[0], halo_sem.at[1])
    for l in range(5):
        cols = slice(128 * l, 128 * l + 128)
        ext[l, 16 : 16 + FR, :] = frames[:, cols].astype(F32)
        ext[l, 0:16, :] = jnp.where(s > 0, halo[0, :, cols].astype(F32), 0.0)
        ext[l, 16 + FR : 32 + FR, :] = jnp.where(s < N_SEQ - 1, halo[1, :, cols].astype(F32), 0.0)
        cwf[l, 0:TAPS, :] = cw[:, cols].astype(F32)

    def conv(i, carry):
        l, rb = i // 8, lax.rem(i, 8)
        r0 = pl.multiple_of(rb * 64, 64)
        acc = jnp.zeros((64, 128), F32)
        for j in range(TAPS):
            acc = acc + ext[l, pl.ds(r0 + (j + 1), 64), :] * cwf[l, pl.ds(j, 1), :]
        act[...] = ext[l, pl.ds(r0 + 16, 64), :] + acc / (1.0 + jnp.exp(-acc))
        total = act[pl.ds(0, 16, stride=4), :]
        for k in range(1, POOL):
            total = total + act[pl.ds(k, 16, stride=4), :]
        pooled[pl.ds(pl.multiple_of(rb * 16, 16), 16), pl.ds(pl.multiple_of(l * 128, 128), 128)] = (
            total * (1.0 / POOL)
        ).astype(BF)
        return carry

    lax.fori_loop(0, 20, conv, 0)

    for part in EARLY:
        turn(f_b, f_c, f_d, f1_sem.at[part[2]], f2_sem, 0, part)
    lax.fori_loop(20, 40, conv, 0)
    plo[v] = mm(pooled[...], chan[...]).astype(BF)
    core_cp = remote(plo.at[v], plo.at[v], pool_s.at[0], pool_r.at[0], other)
    next_cp = remote(plo.at[v], plp.at[v], pool_s.at[1], pool_r.at[1], nxt)
    core_cp.start()

    @pl.when(y < 3)
    def _():
        next_cp.start()

    @pl.when(y == 3)
    def _():
        last = pl.ds(3 * PART, PART)
        remote(plo.at[v, last], plp.at[v, last], pool_s.at[1], pool_r.at[1], ahead).start()
        for i in range(3):
            remote(plo.at[v, pl.ds(i * PART, PART)], passing, pool_s.at[1], pool_r.at[4], at(x, z, i)).start()


    wait_got(wrz.at[pl.ds(0, 80)], wz_sem.at[1])
    sent = wrz.at[pl.ds(0, 112)]
    remote(sent, sent, wz_sem.at[0], wz_sem.at[1], other).wait_send()
    prow80 = pl.multiple_of(p * KB, 16)
    packed = wrz[...]
    for c in range(NC):
        wst[c, 0:64, :] = mm(unpack[64 * c : 64 * c + 64], packed[:, 0:half]).astype(BF)
    for g in range(7):
        piece = mm(unpack[128 + 16 * g : 144 + 16 * g], packed[:, half:]).astype(BF)
        for b in range(2):
            col = 256 * g + 128 * b
            c, off = col // CW, col % CW
            wst[c, 64:KB, off : off + 128] = piece[:, 128 * b : 128 * b + 128]
    mine = lax.rem(x, 2)
    wfull[pl.ds(prow80, KB), :] = wst[mine]

    def wblock(f, g, cols=WHOLE):
        row = pl.multiple_of((lax.rem(x + f, 4) * 4 + lax.rem(y + g, 4)) * KB, 16)
        return wfull.at[pl.ds(row, KB), pl.ds(cols[0], cols[1])]

    def wsend(block, dst, sem, dev):
        remote(block, dst, ws_sem.at[0], sem, dev).start()

    def wsecond(f, part):
        passed, ends = wr_sem.at[part[2], f], wl_sem.at[part[2]]
        up, down = (passed, ends) if f < 2 else (ends, passed)
        wsend(wblock(f, 0, part), wblock(f, 0, part), up, at(x, z, lax.rem(y + 1, 4)))
        wsend(wblock(f, 0, part), wblock(f, 0, part), down, at(x, z, lax.rem(y + 3, 4)))

    def w2relay(f, part):
        near, to = (3, 1) if f < 2 else (1, 3)
        wait_got(wblock(f, near, part), wr_sem.at[part[2], f])
        wsend(wblock(f, near, part), wblock(f, near, part), wl_sem.at[part[2]], at(x, z, lax.rem(y + to, 4)))

    def xpeer(f):
        return at(lax.rem(x + f, 4), z, y)

    for f in (1, 3, 2):
        wsend(wst.at[mine if f == 2 else 1 - mine], wblock(0, 0), w1_sem.at[f], xpeer(f))
    for part in EARLY:
        wsecond(0, part)

    wait_all(idall.at[pl.ds(0, 120)], idp_sem.at[0], idp_sem.at[1])
    dup = []
    for i in range(PLANE):
        piece = idall[8 * i : 8 * i + 8, :]
        dup += [piece, piece]
    every = jnp.concatenate(dup, axis=0)
    lane = lax.broadcasted_iota(jnp.int32, (SLOT, 128), 1)
    rrow = lax.broadcasted_iota(jnp.int32, (SLOT, 128), 0)
    want = lax.rem(z, 4) * 32 + ((rrow >> 3) & 1) * 16 + p
    codes = jnp.sum(jnp.where(lane == want, every, 0).astype(F32), axis=1, keepdims=True).astype(jnp.int32)
    starts = jnp.sum(jnp.where(lane == at_start, every, 0).astype(F32), axis=1, keepdims=True).astype(jnp.int32)
    mrow = lax.broadcasted_iota(jnp.int32, (128, 128), 0)
    mcol = lax.broadcasted_iota(jnp.int32, (128, 128), 1)
    stcol = jnp.sum(jnp.where(mcol == at_start, idall[...], 0).astype(F32), axis=1, keepdims=True)
    strow = jnp.sum(jnp.where(mrow == mcol, stcol, 0.0), axis=0, keepdims=True)
    rcol = lax.broadcasted_iota(jnp.int32, (SLOT, 1), 0)
    rp = rcol >> 4
    rs = ((rp >> 2) * 8 + (rcol & 7)) * 4 + (rp & 3)
    rprev = rs - 1
    prevm = jnp.where(rs == 0, -1, ((rprev >> 5) * 4 + (rprev & 3)) * 8 + ((rprev >> 2) & 7))
    prevst = jnp.sum(jnp.where(lane == prevm, strow, 0.0), axis=1, keepdims=True).astype(jnp.int32)
    prevst = jnp.where(rs == 0, -4096, prevst)
    rslot = rs * SLOT + (codes >> 11)
    audio = ((rslot >= starts) & (rslot < starts + RUN)) | ((rslot >= prevst) & (rslot < prevst + RUN))
    rowid = jnp.where(audio | (codes == 0), -1, (codes & 2047) - 1)
    vi = lax.broadcasted_iota(jnp.int32, (SLOT, VROWS), 1)
    look = jnp.where(vi == rowid, 1.0, 0.0).astype(BF)

    r_a[0] = mm(look, table[:, 0:CW]).astype(BF)
    p_send(r_a, r_b, r1_sem, 0)
    r_a[1] = mm(look, table[:, CW:]).astype(BF)

    rowrow = jnp.sum(jnp.where(diag, rowid.astype(F32), 0.0), axis=0, keepdims=True).astype(jnp.int32)
    sprev = lax.rem(s + N_SEQ - 1, N_SEQ)
    mprev = ((sprev // 32) * 4 + lax.rem(sprev, 4)) * 8 + lax.rem(sprev // 4, 8)
    mlane = lax.broadcasted_iota(jnp.int32, (1, 128), 1)
    before = jnp.sum(jnp.where(mlane == mprev, strow, 0.0), axis=1, keepdims=True).astype(jnp.int32)
    before = jnp.where(s > 0, before, -4096)

    p_send(r_a, r_b, r1_sem, 1)
    @pl.when(y < 3)
    def _():
        part = pl.ds(pl.multiple_of(y * PART, PART), PART)
        wait_got(passing, pool_r.at[4])
        remote(passing, plp.at[v, part], pool_s.at[4], pool_r.at[1], ahead).start()

    turn(f_b, f_c, f_d, f1_sem.at[0], f2_sem, 1)
    for f in (1, 3, 2):
        wait_got(wblock(f, 0), w1_sem.at[4 - f])
        wsecond(f, EARLY[0])
    for f in (1, 3, 2):
        wsecond(f, EARLY[1])

    turn(r_b, r_c, r_d, r1_sem, r2_sem, 0)
    next_cp.wait()
    fwd_cp = remote(plp.at[v], plp.at[v], pool_s.at[2], pool_r.at[2], other)
    fwd_cp.start()
    for part in EARLY:
        w2relay(0, part)

    core_cp.wait()
    fwd_cp.wait()
    def xsend(src, dst, sem, f):
        remote(src, dst, sem.at[0], sem.at[1], xpeer(f)).start()

    qslot = s * SLOT + lax.broadcasted_iota(jnp.int32, (SLOT, RUN), 0)
    prun = lax.broadcasted_iota(jnp.int32, (SLOT, RUN), 1)
    own_sel = jnp.where(qslot == start + prun, 1.0, 0.0).astype(BF)
    prev_sel = jnp.where(qslot == before + prun, 1.0, 0.0).astype(BF)
    for h in range(2):
        xs[h, 0:SLOT, :] = (mm(own_sel, plo[h]) + mm(prev_sel, plp[h])).astype(BF)
    xsend(xs.at[v, pl.ds(0, RUN)], xs.at[v, pl.ds(SLOT, RUN)], xx_sem, 1)
    xsend(xs.at[v, pl.ds(RUN, RUN)], xs.at[v, pl.ds(SLOT + RUN, RUN)], xx_sem, 3)

    turn(r_b, r_c, r_d, r1_sem, r2_sem, 1)
    for part in EARLY:
        for f in (1, 3, 2):
            w2relay(f, part)

    wait_all(xs.at[v, pl.ds(SLOT, SLOT)], xx_sem.at[0], xx_sem.at[1])
    x_cp = remote(xs.at[v, pl.ds(SLOT, SLOT)], xs.at[v, pl.ds(SLOT, SLOT)], pool_s.at[3], pool_r.at[3], other)
    x_cp.start()

    for c in range(NC):
        z_wait(f_d, f2_sem, c)
    got_cps = []
    for c in range(NC):
        f_c[c] = mm(relay[...], f_d[c]).astype(BF)
        got_cps.append(pltpu.make_async_copy(f_c.at[c], got_out.at[:, pl.ds(c * CW, CW)], loc_sem.at[2 + c]))
        got_cps[-1].start()
    row_ref[...] = jnp.broadcast_to(rowrow, (8, SLOT))
    vrow = lax.broadcasted_iota(jnp.int32, (VROWS, SLOT), 0)
    place[...] = jnp.where(vrow == rowrow, 1.0, 0.0).astype(BF)

    def gtile(i, carry):
        cols = pl.ds(pl.multiple_of(i * TILE, TILE), TILE)
        gpre[:, cols] = mm(place[...], f_c[0, :, cols]).astype(BF)
        return carry

    lax.fori_loop(0, PRE, gtile, 0)
    got_cps.append(pltpu.make_async_copy(gpre, gpre_out, loc_sem.at[4]))
    got_cps[-1].start()
    x_cp.wait()
    for part in EARLY:
        cols = pl.ds(part[0], part[1])
        wait_got(wfull.at[pl.ds(0, 8 * KB), cols], wl_sem.at[part[2]])
        far[:, cols] = (mm(xs[0, SLOT:, :], wfull[0:CH, cols]) + mm(xs[1, SLOT:, :], wfull[CH:, cols])).astype(BF)
        xsend(far.at[pl.ds(0, RUN), cols], opp.at[pl.ds(0, RUN), cols], xo_sem, 3)
        xsend(far.at[pl.ds(RUN, RUN), cols], opp.at[pl.ds(RUN, RUN), cols], xo_sem, 1)
        llm[mine, :, cols] = (
            mm(xs[0, 0:SLOT, :], wfull[0:CH, cols]) + mm(xs[1, 0:SLOT, :], wfull[CH:, cols])
        ).astype(BF)
    for c in range(NC):
        z_wait(r_d, r2_sem, c)
        text[c] = lax.dot_general(
            sel_s[...], r_d[c], (((0,), (0,)), ((), ())), preferred_element_type=F32
        ).astype(BF)
    llm[mine] = (llm[mine].astype(F32) + text[mine].astype(F32)).astype(BF)
    outs = [pltpu.make_async_copy(llm.at[mine], llm_out.at[mine], loc_sem.at[0])]
    outs[0].start()
    wait_all(opp, xo_sem.at[0], xo_sem.at[1])
    llm[1 - mine] = (opp[...].astype(F32) + text[1 - mine].astype(F32)).astype(BF)
    outs.append(pltpu.make_async_copy(llm.at[1 - mine], llm_out.at[1 - mine], loc_sem.at[1]))
    outs[1].start()
    @pl.when(y < 3)
    def _():
        remote(passing, passing, pool_s.at[4], pool_r.at[4], other).wait_send()

    block = wfull.at[pl.ds(0, 15 * KB)]
    remote(block, block, ws_sem.at[0], wl_sem.at[0], other).wait_send()
    for cp in got_cps:
        cp.wait()
    for cp in outs:
        cp.wait()


def write_kernel(
    row_hbm, got_hbm, llm_hbm, ready_hbm, out_hbm, grad_hbm, row, got, llm, ready, grad, place, in_sem, out_sem
):
    tiles = D // TILE

    def get(i):
        cols = pl.ds(pl.multiple_of(i * TILE, TILE), TILE)
        return pltpu.make_async_copy(got_hbm.at[:, cols], got.at[i], in_sem.at[i])

    def put(i):
        cols = pl.ds(pl.multiple_of(i * TILE, TILE), TILE)
        return pltpu.make_async_copy(grad.at[i], grad_hbm.at[:, cols], out_sem.at[i])

    def put_llm(h):
        return pltpu.make_async_copy(llm.at[h], out_hbm.at[:, pl.ds(h * CW, CW)], out_sem.at[tiles + h])

    row_cp = pltpu.make_async_copy(row_hbm, row, in_sem.at[tiles])
    row_cp.start()
    llm_in = pltpu.make_async_copy(llm_hbm, llm, in_sem.at[tiles + 1])
    for i in range(PRE, tiles):
        get(i).start()
    ready_in = pltpu.make_async_copy(ready_hbm, ready, in_sem.at[0])
    ready_in.start()
    ready_out = pltpu.make_async_copy(ready, grad_hbm.at[:, pl.ds(0, PRE * TILE)], out_sem.at[0])
    llm_in.start()
    row_cp.wait()
    vi = lax.broadcasted_iota(jnp.int32, (VROWS, SLOT), 0)
    place[...] = jnp.where(vi == row[0:1, :], 1.0, 0.0).astype(BF)

    def tile(i, c):
        get(i).wait()
        grad[i] = mm(place[...], got[i]).astype(BF)
        put(i).start()
        return c

    lax.fori_loop(PRE, PRE + 1, tile, 0)
    ready_in.wait()
    ready_out.start()
    lax.fori_loop(PRE + 1, tiles, tile, 0)
    llm_in.wait()
    for h in range(NC):
        put_llm(h).start()
    for i in range(PRE, tiles):
        put(i).wait()
    ready_out.wait()
    for h in range(NC):
        put_llm(h).wait()


def shards(frames, conv_weight, proj_weight, table, audio_pos, token_ids, cotangent):
    relay = relay_matrix()
    consts = [relay, relay.T, channel_matrix(), pack_matrices(), unpack_matrices()]
    consts = [jnp.asarray(m, dtype=BF) for m in consts]
    hbm = pl.BlockSpec(memory_space=pltpu.HBM)
    anywhere = pl.BlockSpec(memory_space=pl.ANY)
    dma = pltpu.SemaphoreType.DMA
    wide = pltpu.VMEM((NC, SLOT, CW), BF)
    llm, got, ready, rows = pl.pallas_call(
        comm_kernel,
        out_shape=[
            jax.ShapeDtypeStruct((NC, SLOT, CW), BF),
            jax.ShapeDtypeStruct((SLOT, D), BF),
            jax.ShapeDtypeStruct((VROWS, PRE * TILE), BF),
            jax.ShapeDtypeStruct((8, SLOT), jnp.int32),
        ],
        in_specs=[hbm] * 12,
        out_specs=[anywhere, anywhere, anywhere, pl.BlockSpec(memory_space=pltpu.VMEM)],
        scratch_shapes=[
            pltpu.VMEM((1, SLOT), jnp.int32),
            pltpu.VMEM((1, RUN), jnp.int32),
            pltpu.VMEM((FR, CH), BF),
            pltpu.VMEM((TAPS, CH), BF),
            pltpu.VMEM((WROWS, D), BF),
            pltpu.VMEM((SLOT, SLOT), BF),
            pltpu.VMEM((SLOT, SLOT), BF),
            pltpu.VMEM((CH, CH), BF),
            pltpu.VMEM((144, 16), BF),
            pltpu.VMEM((240, 128), BF),
            pltpu.VMEM((SLOT, D), BF),
            pltpu.VMEM((VROWS, D), BF),
            pltpu.VMEM((SLOT, SLOT), BF),
            wide, wide, wide, wide, wide, wide, wide, wide,
            pltpu.VMEM((8, 128), jnp.int32),
            pltpu.VMEM((64, 128), jnp.int32),
            pltpu.VMEM((8, 128), jnp.int32),
            pltpu.VMEM((128, 128), jnp.int32),
            pltpu.VMEM((2, 16, CH), BF),
            pltpu.VMEM((5, FR + 32, 128), F32),
            pltpu.VMEM((5, 32, 128), F32),
            pltpu.VMEM((64, 128), F32),
            pltpu.VMEM((RUN, CH), BF),
            pltpu.VMEM((2, RUN, CH), BF),
            pltpu.VMEM((2, RUN, CH), BF),
            pltpu.VMEM((16, D), F32),
            pltpu.VMEM((16, WP), BF),
            pltpu.VMEM((128, WP), BF),
            pltpu.VMEM((NC, KB, CW), BF),
            pltpu.VMEM((PLANE * KB, CW), BF),
            pltpu.VMEM((2, 2 * SLOT, CH), BF),
            pltpu.VMEM((SLOT, CW), BF),
            pltpu.VMEM((SLOT, CW), BF),
            wide, wide,
            pltpu.VMEM((PART, CH), BF),
            pltpu.VMEM((VROWS, SLOT), BF),
            pltpu.VMEM((VROWS, PRE * TILE), BF),
            dma((12,)), dma((2,)), dma((2,)), dma((2,)), dma((7,)),
            dma((2, 2, 2)), dma((2, 2)), dma((2, 2)), dma((2, 2)),
            dma((1,)), dma((4,)), dma((2, 4)), dma((2,)), dma((5,)), dma((5,)), dma((2,)), dma((2,)),
        ],
        compiler_params=pltpu.CompilerParams(
            collective_id=0, has_side_effects=True, vmem_limit_bytes=VMEM_LIMIT
        ),
        name="exchange",
    )(
        token_ids.reshape(1, SLOT), audio_pos.reshape(1, RUN), frames, conv_weight, proj_weight, *consts,
        cotangent, table,
    )
    return pl.pallas_call(
        write_kernel,
        out_shape=[jax.ShapeDtypeStruct((SLOT, D), BF), jax.ShapeDtypeStruct((VROWS, D), BF)],
        in_specs=[hbm] * 4,
        out_specs=[anywhere, anywhere],
        scratch_shapes=[
            pltpu.VMEM((8, SLOT), jnp.int32),
            pltpu.VMEM((D // TILE, SLOT, TILE), BF),
            wide,
            pltpu.VMEM((VROWS, PRE * TILE), BF),
            pltpu.VMEM((D // TILE, VROWS, TILE), BF),
            pltpu.VMEM((VROWS, SLOT), BF),
            dma((D // TILE + 2,)),
            dma((D // TILE + 2,)),
        ],
        compiler_params=pltpu.CompilerParams(vmem_limit_bytes=VMEM_LIMIT),
        name="write",
    )(rows, got, llm, ready)


def solution(mesh):
    return jax.shard_map(
        shards,
        mesh=mesh,
        in_specs=(
            P("seq", "vocab"),
            P(None, "vocab"),
            P("seq", "vocab"),
            P("seq", "vocab"),
            P("seq"),
            P("seq"),
            P("seq", "vocab"),
        ),
        out_specs=(P("seq", "vocab"), P("seq", "vocab")),
        check_vma=False,
    )
```

```python
import functools

import jax
import jax.numpy as jnp
import numpy as np
from jax import lax
from jax.experimental import pallas as pl
from jax.experimental.pallas import tpu as pltpu
from jax.sharding import PartitionSpec as P

MESH = pl.DeviceIdType.MESH
BF = jnp.bfloat16
F32 = jnp.float32
NX, NZ, NY = 4, 8, 4
N_SEQ = NX * NZ * NY
PLANE = NX * NY
POOL = 4
SLOT = 256
RUN = 128
PART = 32
VROWS = 1188
D = 1792
NC = 2
CW = D // NC
WHOLE = (0, CW)
EARLY = ((0, 384, 0), (384, 512, 1))
CH = 640
FR = 512
TAPS = 31
WROWS = 10
WP = 1152
KB = NZ * WROWS
TILE = 256
PRE = 5
VMEM_LIMIT = 60 * 1024 * 1024


def relay_matrix():
    m = np.zeros((SLOT, SLOT), np.float32)
    for z in range(NZ):
        for k in range(2):
            for p in range(PLANE):
                m[p * 16 + k * 8 + z, z * 32 + k * 16 + p] = 1
    return m


def channel_matrix():
    m = np.zeros((CH, CH), np.float32)
    for c in range(CH):
        x, z, y, i = c // 320, (c % 320) // 40, (c % 40) // 10, c % 10
        inner = z * 8 + i if i < 8 else 64 + z * 2 + i - 8
        m[c, (x * 4 + y) * KB + inner] = 1
    return m


def pack_matrices():
    m = np.zeros((9, 16, 16), np.float32)
    for i in range(8):
        m[0, i, i] = 1
        m[1, 8 + i, i] = 1
    for g in range(7):
        for i in range(2):
            m[2 + g, 2 * g + i, 8 + i] = 1
    return m.reshape(9 * 16, 16)


def unpack_matrices():
    top = np.zeros((2, 64, 128), np.float32)
    low = np.zeros((7, 16, 128), np.float32)
    for z in range(NZ):
        for i in range(8):
            top[0, z * 8 + i, z * 16 + i] = 1
            top[1, z * 8 + i, z * 16 + 8 + i] = 1
        for g in range(7):
            for i in range(2):
                low[g, z * 2 + i, z * 16 + 2 * g + i] = 1
    return np.concatenate([top.reshape(128, 128), low.reshape(112, 128)])


def mm(a, b):
    return jnp.dot(a, b, preferred_element_type=F32)


def comm_kernel(
    ids_hbm, pos_hbm, frames_hbm, cw_hbm, w_hbm, relay_hbm, back_hbm, chan_hbm, pack_hbm, unpack_hbm,
    cot_hbm, table_hbm,
    llm_out, got_out, gpre_out, row_ref,
    ids_ref, pos_ref, frames, cw, wown, relay, backm, chan, pack, unpack,
    cot, table, sel_s, f_a, f_b, f_c, f_d, r_a, r_b, r_c, r_d,
    idsnd, idrcv, idcomp, idall, halo, ext, cwf, act, pooled, plo, plp,
    wpadf, wpk, wrz, wst, wfull, xs, far, opp, text, llm, passing, place, gpre, gotv,
    loc_sem, halo_sem, idz_sem, idp_sem, wz_sem,
    f1_sem, f2_sem, r1_sem, r2_sem,
    ws_sem, w1_sem, wr_sem, wl_sem, pool_s, pool_r, xx_sem, xo_sem,
):
    s = lax.axis_index("seq")
    v = lax.axis_index("vocab")
    x, z, y = s // 32, (s // 4) % 8, s % 4
    p = x * 4 + y

    def at(xx, zz, yy):
        return ((xx * 8 + zz) * 4 + yy, v)

    def zpeer(d):
        return at(x, lax.rem(z + d, 8), y)

    def ppeer(j):
        return at(lax.rem(x + j // 4, 4), z, lax.rem(y + lax.rem(j, 4), 4))

    def pplace(j):
        return lax.rem(x + j // 4, 4) * 4 + lax.rem(y + lax.rem(j, 4), 4)

    nxt = (lax.rem(s + 1, N_SEQ), v)
    prv = (lax.rem(s + N_SEQ - 1, N_SEQ), v)
    other = (s, 1 - v)
    ahead = (lax.rem((s // 4 + 1) * 4, N_SEQ), v)

    def behind(i):
        return (lax.rem(s + N_SEQ - 4 + i, N_SEQ), v)


    def remote(src, dst, ss, rs, dev):
        return pltpu.make_async_remote_copy(
            src_ref=src, dst_ref=dst, send_sem=ss, recv_sem=rs, device_id=dev, device_id_type=MESH
        )

    def wait_all(block, ss, rs):
        cp = remote(block, block, ss, rs, other)
        cp.wait_send()
        cp.wait_recv()

    def wait_got(block, rs):
        remote(block, block, ws_sem.at[0], rs, other).wait_recv()

    def plane(fn):
        def body(j, c):
            fn(j)
            return c

        lax.fori_loop(1, PLANE, body, 0)

    prow16 = pl.multiple_of(p * 16, 16)
    zrow = pl.multiple_of(z * 32, 32)

    def z_send(src, dst, sem, c, part=WHOLE):
        cols = pl.ds(part[0], part[1])
        for d in (4, 3, 5, 2, 6, 1, 7):
            to = pl.multiple_of(lax.rem(z + d, 8) * 32, 32)
            remote(
                src.at[c, pl.ds(to, 32), cols], dst.at[c, pl.ds(zrow, 32), cols], sem.at[0, c], sem.at[1, c], zpeer(d)
            ).start()
        dst[c, pl.ds(zrow, 32), cols] = src[c, pl.ds(zrow, 32), cols]

    def p_send(src, dst, sem, c, part=WHOLE):
        cols = pl.ds(part[0], part[1])

        def send(j):
            to = pl.multiple_of(pplace(j) * 16, 16)
            remote(
                src.at[c, pl.ds(to, 16), cols], dst.at[c, pl.ds(prow16, 16), cols], sem.at[0, c], sem.at[1, c], ppeer(j)
            ).start()

        plane(send)
        dst[c, pl.ds(prow16, 16), cols] = src[c, pl.ds(prow16, 16), cols]

    def z_wait(dst, sem, c):
        wait_all(dst.at[c, pl.ds(0, 224)], sem.at[0, c], sem.at[1, c])

    def p_wait(dst, sem, c, part=WHOLE):
        wait_all(dst.at[c, pl.ds(0, 240), pl.ds(part[0], part[1])], sem.at[0, c], sem.at[1, c])

    def turn(first, mid, last, sem1, sem2, c, part=WHOLE):
        cols = pl.ds(part[0], part[1])
        p_wait(first, sem1, c, part)
        mid[c, :, cols] = mm(backm[...], first[c, :, cols]).astype(BF)
        z_send(mid, last, sem2, c, part)

    bar = pltpu.get_barrier_semaphore()
    for d in (4, 3, 5, 2, 6, 1, 7):
        pl.semaphore_signal(bar, inc=1, device_id=zpeer(d), device_id_type=MESH)
    plane(lambda j: pl.semaphore_signal(bar, inc=1, device_id=ppeer(j), device_id_type=MESH))
    for dev in (nxt, prv, other, ahead):
        pl.semaphore_signal(bar, inc=1, device_id=dev, device_id_type=MESH)

    @pl.when(y == 0)
    def _():
        for i in range(4):
            pl.semaphore_signal(bar, inc=1, device_id=behind(i), device_id_type=MESH)


    local = {}
    for i, (name, src, dst) in enumerate(
        (
            ("ids", ids_hbm, ids_ref), ("pos", pos_hbm, pos_ref), ("w", w_hbm, wown), ("pack", pack_hbm, pack),
            ("frames", frames_hbm, frames), ("cot", cot_hbm, cot), ("relay", relay_hbm, relay), ("cw", cw_hbm, cw),
            ("unpack", unpack_hbm, unpack), ("back", back_hbm, backm), ("table", table_hbm, table),
            ("chan", chan_hbm, chan),
        )
    ):
        local[name] = pltpu.make_async_copy(src, dst, loc_sem.at[i])
        local[name].start()

    local["ids"].wait()
    local["pos"].wait()
    bcol = lax.broadcasted_iota(jnp.int32, (SLOT, 1), 0)
    bz, bk, bp = bcol >> 5, (bcol >> 4) & 1, bcol & 15
    low = (((bp >> 2) * 8 + bz) * 4 + (bp & 3)) * VROWS
    rel = ids_ref[...] - low
    qint = lax.broadcasted_iota(jnp.int32, (SLOT, SLOT), 1)
    qi = qint.astype(F32)
    hit = (rel >= 0) & (rel < VROWS)
    first = jnp.min(jnp.where(hit, qi, 4096.0), axis=1, keepdims=True)
    last = jnp.max(jnp.where(hit, qi, -1.0), axis=1, keepdims=True)
    chosen = jnp.where(bk == 0, first, jnp.where(last > first, last, -1.0))
    picked = qi == chosen
    sel_s[...] = jnp.where(picked, 1.0, 0.0).astype(BF)
    code = jnp.sum(jnp.where(picked, (qint * 2048 + rel + 1).astype(F32), 0.0), axis=1, keepdims=True)
    brow = lax.broadcasted_iota(jnp.int32, (SLOT, SLOT), 0)
    diag = brow == qint
    coderow = jnp.sum(jnp.where(diag, code, 0.0), axis=0, keepdims=True).astype(jnp.int32)
    start = pos_ref[0:1, 0:1]
    eight = lax.broadcasted_iota(jnp.int32, (8, 128), 0)
    idsnd[...] = jnp.where(
        eight == 0, coderow[:, 0:128], jnp.where(eight == 1, coderow[:, 128:256], jnp.broadcast_to(start, (8, 128)))
    )
    zrow8 = pl.multiple_of(z * 8, 8)
    idrcv[pl.ds(zrow8, 8), :] = idsnd[...]

    local["w"].wait()
    local["pack"].wait()
    wpadf[...] = jnp.zeros_like(wpadf)
    wpadf[0:WROWS, :] = wown[...].astype(F32)
    wp = wpadf[...].astype(BF)
    half = D // 2
    wpk[:, 0:half] = (mm(pack[0:16], wp[:, 0:half]) + mm(pack[16:32], wp[:, half:])).astype(BF)
    tail = jnp.zeros((16, 256), F32)
    for g in range(7):
        tail = tail + mm(pack[32 + 16 * g : 48 + 16 * g], wp[:, 256 * g : 256 * g + 256])
    wpk[:, half:] = tail.astype(BF)
    zrow16 = pl.multiple_of(z * 16, 16)
    wrz[pl.ds(zrow16, 16), :] = wpk[...]

    local["cot"].wait()
    local["relay"].wait()

    def bucketed(c):
        f_a[c] = mm(relay[...], mm(sel_s[...], cot[:, c * CW : (c + 1) * CW]).astype(BF)).astype(BF)

    bucketed(0)
    local["frames"].wait()

    @pl.when(y == 0)
    def _():
        pl.semaphore_wait(bar, 7 + PLANE - 1 + 8)

    @pl.when(y > 0)
    def _():
        pl.semaphore_wait(bar, 7 + PLANE - 1 + 4)


    for d in (1, 7, 2, 6, 3, 5, 4):
        remote(idsnd, idrcv.at[pl.ds(zrow8, 8)], idz_sem.at[0], idz_sem.at[1], zpeer(d)).start()
    remote(frames.at[pl.ds(FR - 16, 16)], halo.at[0], halo_sem.at[0], halo_sem.at[1], nxt).start()
    remote(frames.at[pl.ds(0, 16)], halo.at[1], halo_sem.at[0], halo_sem.at[1], prv).start()
    def ring_block(k):
        return wrz.at[pl.ds(pl.multiple_of(lax.rem(z + k, 8) * 16, 16), 16)]

    for d in (2, 6, 1, 7):
        remote(wpk, ring_block(0), wz_sem.at[0], wz_sem.at[1 if d in (1, 7) else d], zpeer(d)).start()
    for part in EARLY:
        p_send(f_a, f_b, f1_sem.at[part[2]], 0, part)
    bucketed(1)
    for name in ("cw", "unpack", "back", "table", "chan"):
        local[name].wait()

    wait_all(idrcv.at[pl.ds(0, 56)], idz_sem.at[0], idz_sem.at[1])
    even = idrcv[pl.ds(0, 8, stride=8), :]
    odd = idrcv[pl.ds(1, 8, stride=8), :]
    lane8 = lax.broadcasted_iota(jnp.int32, (8, 128), 1)
    at_start = lax.rem(z + 1, 4) * 32
    idcomp[...] = jnp.where(lane8 == at_start, idrcv[pl.ds(2, 8, stride=8), :], jnp.where(z < 4, even, odd))
    prow8 = pl.multiple_of(p * 8, 8)
    idall[pl.ds(prow8, 8), :] = idcomp[...]
    plane(
        lambda j: remote(idcomp, idall.at[pl.ds(prow8, 8)], idp_sem.at[0], idp_sem.at[1], ppeer(j)).start()
    )
    p_send(f_a, f_b, f1_sem.at[0], 1)

    wait_got(ring_block(6), wz_sem.at[2])
    remote(ring_block(6), ring_block(6), wz_sem.at[0], wz_sem.at[1], zpeer(1)).start()
    remote(ring_block(6), ring_block(6), wz_sem.at[0], wz_sem.at[1], zpeer(2)).start()
    wait_got(ring_block(2), wz_sem.at[6])
    remote(ring_block(2), ring_block(2), wz_sem.at[0], wz_sem.at[1], zpeer(7)).start()
    wait_all(halo, halo_sem.at[0], halo_sem.at[1])
    for l in range(5):
        cols = slice(128 * l, 128 * l + 128)
        ext[l, 16 : 16 + FR, :] = frames[:, cols].astype(F32)
        ext[l, 0:16, :] = jnp.where(s > 0, halo[0, :, cols].astype(F32), 0.0)
        ext[l, 16 + FR : 32 + FR, :] = jnp.where(s < N_SEQ - 1, halo[1, :, cols].astype(F32), 0.0)
        cwf[l, 0:TAPS, :] = cw[:, cols].astype(F32)

    def conv(i, carry):
        l, rb = i // 8, lax.rem(i, 8)
        r0 = pl.multiple_of(rb * 64, 64)
        acc = jnp.zeros((64, 128), F32)
        for j in range(TAPS):
            acc = acc + ext[l, pl.ds(r0 + (j + 1), 64), :] * cwf[l, pl.ds(j, 1), :]
        act[...] = ext[l, pl.ds(r0 + 16, 64), :] + acc / (1.0 + jnp.exp(-acc))
        total = act[pl.ds(0, 16, stride=4), :]
        for k in range(1, POOL):
            total = total + act[pl.ds(k, 16, stride=4), :]
        pooled[pl.ds(pl.multiple_of(rb * 16, 16), 16), pl.ds(pl.multiple_of(l * 128, 128), 128)] = (
            total * (1.0 / POOL)
        ).astype(BF)
        return carry

    lax.fori_loop(0, 10, conv, 0)

    turn(f_b, f_c, f_d, f1_sem.at[0], f2_sem, 0, EARLY[0])
    lax.fori_loop(10, 20, conv, 0)
    turn(f_b, f_c, f_d, f1_sem.at[1], f2_sem, 0, EARLY[1])
    lax.fori_loop(20, 40, conv, 0)
    plo[v] = mm(pooled[...], chan[...]).astype(BF)
    core_cp = remote(plo.at[v], plo.at[v], pool_s.at[0], pool_r.at[0], other)
    next_cp = remote(plo.at[v], plp.at[v], pool_s.at[1], pool_r.at[1], nxt)
    core_cp.start()

    @pl.when(y < 3)
    def _():
        next_cp.start()

    @pl.when(y == 3)
    def _():
        last = pl.ds(3 * PART, PART)
        remote(plo.at[v, last], plp.at[v, last], pool_s.at[1], pool_r.at[1], ahead).start()
        for i in range(3):
            remote(plo.at[v, pl.ds(i * PART, PART)], passing, pool_s.at[1], pool_r.at[4], at(x, z, i)).start()


    wait_all(idall.at[pl.ds(0, 120)], idp_sem.at[0], idp_sem.at[1])
    dup = []
    for i in range(PLANE):
        piece = idall[8 * i : 8 * i + 8, :]
        dup += [piece, piece]
    every = jnp.concatenate(dup, axis=0)
    lane = lax.broadcasted_iota(jnp.int32, (SLOT, 128), 1)
    rrow = lax.broadcasted_iota(jnp.int32, (SLOT, 128), 0)
    want = lax.rem(z, 4) * 32 + ((rrow >> 3) & 1) * 16 + p
    codes = jnp.sum(jnp.where(lane == want, every, 0).astype(F32), axis=1, keepdims=True).astype(jnp.int32)
    starts = jnp.sum(jnp.where(lane == at_start, every, 0).astype(F32), axis=1, keepdims=True).astype(jnp.int32)
    mrow = lax.broadcasted_iota(jnp.int32, (128, 128), 0)
    mcol = lax.broadcasted_iota(jnp.int32, (128, 128), 1)
    stcol = jnp.sum(jnp.where(mcol == at_start, idall[...], 0).astype(F32), axis=1, keepdims=True)
    strow = jnp.sum(jnp.where(mrow == mcol, stcol, 0.0), axis=0, keepdims=True)
    rcol = lax.broadcasted_iota(jnp.int32, (SLOT, 1), 0)
    rp = rcol >> 4
    rs = ((rp >> 2) * 8 + (rcol & 7)) * 4 + (rp & 3)
    rprev = rs - 1
    prevm = jnp.where(rs == 0, -1, ((rprev >> 5) * 4 + (rprev & 3)) * 8 + ((rprev >> 2) & 7))
    prevst = jnp.sum(jnp.where(lane == prevm, strow, 0.0), axis=1, keepdims=True).astype(jnp.int32)
    prevst = jnp.where(rs == 0, -4096, prevst)
    rslot = rs * SLOT + (codes >> 11)
    audio = ((rslot >= starts) & (rslot < starts + RUN)) | ((rslot >= prevst) & (rslot < prevst + RUN))
    rowid = jnp.where(audio | (codes == 0), -1, (codes & 2047) - 1)
    vi = lax.broadcasted_iota(jnp.int32, (SLOT, VROWS), 1)
    look = jnp.where(vi == rowid, 1.0, 0.0).astype(BF)

    for part in EARLY:
        cols = pl.ds(part[0], part[1])
        r_a[0, :, cols] = mm(look, table[:, cols]).astype(BF)
        p_send(r_a, r_b, r1_sem.at[part[2]], 0, part)
    r_a[1] = mm(look, table[:, CW:]).astype(BF)

    rowrow = jnp.sum(jnp.where(diag, rowid.astype(F32), 0.0), axis=0, keepdims=True).astype(jnp.int32)
    sprev = lax.rem(s + N_SEQ - 1, N_SEQ)
    mprev = ((sprev // 32) * 4 + lax.rem(sprev, 4)) * 8 + lax.rem(sprev // 4, 8)
    mlane = lax.broadcasted_iota(jnp.int32, (1, 128), 1)
    before = jnp.sum(jnp.where(mlane == mprev, strow, 0.0), axis=1, keepdims=True).astype(jnp.int32)
    before = jnp.where(s > 0, before, -4096)

    wait_got(wrz.at[pl.ds(0, 80)], wz_sem.at[1])
    sent = wrz.at[pl.ds(0, 112)]
    remote(sent, sent, wz_sem.at[0], wz_sem.at[1], other).wait_send()
    prow80 = pl.multiple_of(p * KB, 16)
    packed = wrz[...]
    for c in range(NC):
        wst[c, 0:64, :] = mm(unpack[64 * c : 64 * c + 64], packed[:, 0:half]).astype(BF)
    for g in range(7):
        piece = mm(unpack[128 + 16 * g : 144 + 16 * g], packed[:, half:]).astype(BF)
        for b in range(2):
            col = 256 * g + 128 * b
            c, off = col // CW, col % CW
            wst[c, 64:KB, off : off + 128] = piece[:, 128 * b : 128 * b + 128]
    mine = lax.rem(x, 2)
    wfull[pl.ds(prow80, KB), :] = wst[mine]

    def wblock(f, g, cols=WHOLE):
        row = pl.multiple_of((lax.rem(x + f, 4) * 4 + lax.rem(y + g, 4)) * KB, 16)
        return wfull.at[pl.ds(row, KB), pl.ds(cols[0], cols[1])]

    def wsend(block, dst, sem, dev):
        remote(block, dst, ws_sem.at[0], sem, dev).start()

    def wsecond(f, part):
        passed, ends = wr_sem.at[part[2], f], wl_sem.at[part[2]]
        up, down = (passed, ends) if f < 2 else (ends, passed)
        wsend(wblock(f, 0, part), wblock(f, 0, part), up, at(x, z, lax.rem(y + 1, 4)))
        wsend(wblock(f, 0, part), wblock(f, 0, part), down, at(x, z, lax.rem(y + 3, 4)))

    def w2relay(f, part):
        near, to = (3, 1) if f < 2 else (1, 3)
        wait_got(wblock(f, near, part), wr_sem.at[part[2], f])
        wsend(wblock(f, near, part), wblock(f, near, part), wl_sem.at[part[2]], at(x, z, lax.rem(y + to, 4)))

    def xpeer(f):
        return at(lax.rem(x + f, 4), z, y)

    for f in (1, 3, 2):
        wsend(wst.at[mine if f == 2 else 1 - mine], wblock(0, 0), w1_sem.at[f], xpeer(f))
    for part in EARLY:
        wsecond(0, part)

    p_send(r_a, r_b, r1_sem.at[0], 1)
    @pl.when(y < 3)
    def _():
        part = pl.ds(pl.multiple_of(y * PART, PART), PART)
        wait_got(passing, pool_r.at[4])
        remote(passing, plp.at[v, part], pool_s.at[4], pool_r.at[1], ahead).start()

    turn(f_b, f_c, f_d, f1_sem.at[0], f2_sem, 1)
    for f in (1, 3, 2):
        wait_got(wblock(f, 0), w1_sem.at[4 - f])
        wsecond(f, EARLY[0])
    for f in (1, 3, 2):
        wsecond(f, EARLY[1])

    for part in EARLY:
        turn(r_b, r_c, r_d, r1_sem.at[part[2]], r2_sem, 0, part)
    next_cp.wait()
    fwd_cp = remote(plp.at[v], plp.at[v], pool_s.at[2], pool_r.at[2], other)
    fwd_cp.start()
    for part in EARLY:
        w2relay(0, part)

    core_cp.wait()
    fwd_cp.wait()
    def xsend(src, dst, sem, f):
        remote(src, dst, sem.at[0], sem.at[1], xpeer(f)).start()

    qslot = s * SLOT + lax.broadcasted_iota(jnp.int32, (SLOT, RUN), 0)
    prun = lax.broadcasted_iota(jnp.int32, (SLOT, RUN), 1)
    own_sel = jnp.where(qslot == start + prun, 1.0, 0.0).astype(BF)
    prev_sel = jnp.where(qslot == before + prun, 1.0, 0.0).astype(BF)
    for h in range(2):
        xs[h, 0:SLOT, :] = (mm(own_sel, plo[h]) + mm(prev_sel, plp[h])).astype(BF)
    xsend(xs.at[v, pl.ds(0, RUN)], xs.at[v, pl.ds(SLOT, RUN)], xx_sem, 1)
    xsend(xs.at[v, pl.ds(RUN, RUN)], xs.at[v, pl.ds(SLOT + RUN, RUN)], xx_sem, 3)

    turn(r_b, r_c, r_d, r1_sem.at[0], r2_sem, 1)
    for part in EARLY:
        for f in (1, 3, 2):
            w2relay(f, part)

    wait_all(xs.at[v, pl.ds(SLOT, SLOT)], xx_sem.at[0], xx_sem.at[1])
    x_cp = remote(xs.at[v, pl.ds(SLOT, SLOT)], xs.at[v, pl.ds(SLOT, SLOT)], pool_s.at[3], pool_r.at[3], other)
    x_cp.start()

    for c in range(NC):
        z_wait(f_d, f2_sem, c)
    got_cps = []
    for c in range(NC):
        gotv[:, c * CW : (c + 1) * CW] = mm(relay[...], f_d[c]).astype(BF)
    got_cps.append(pltpu.make_async_copy(gotv, got_out, loc_sem.at[2]))
    got_cps[-1].start()
    row_ref[...] = jnp.broadcast_to(rowrow, (8, SLOT))
    vrow = lax.broadcasted_iota(jnp.int32, (VROWS, SLOT), 0)
    place[...] = jnp.where(vrow == rowrow, 1.0, 0.0).astype(BF)

    def gtile(i, carry):
        cols = pl.ds(pl.multiple_of(i * TILE, TILE), TILE)
        gpre[i] = mm(place[...], gotv[:, cols]).astype(BF)
        return carry

    lax.fori_loop(0, PRE, gtile, 0)
    got_cps.append(pltpu.make_async_copy(gpre, gpre_out, loc_sem.at[4]))
    got_cps[-1].start()
    x_cp.wait()
    for part in EARLY:
        cols = pl.ds(part[0], part[1])
        wait_got(wfull.at[pl.ds(0, 8 * KB), cols], wl_sem.at[part[2]])
        far[:, cols] = (mm(xs[0, SLOT:, :], wfull[0:CH, cols]) + mm(xs[1, SLOT:, :], wfull[CH:, cols])).astype(BF)
        xsend(far.at[pl.ds(0, RUN), cols], opp.at[pl.ds(0, RUN), cols], xo_sem, 3)
        xsend(far.at[pl.ds(RUN, RUN), cols], opp.at[pl.ds(RUN, RUN), cols], xo_sem, 1)
        llm[mine, :, cols] = (
            mm(xs[0, 0:SLOT, :], wfull[0:CH, cols]) + mm(xs[1, 0:SLOT, :], wfull[CH:, cols])
        ).astype(BF)
    for c in range(NC):
        z_wait(r_d, r2_sem, c)
        text[c] = lax.dot_general(
            sel_s[...], r_d[c], (((0,), (0,)), ((), ())), preferred_element_type=F32
        ).astype(BF)
    llm[mine] = (llm[mine].astype(F32) + text[mine].astype(F32)).astype(BF)
    outs = [pltpu.make_async_copy(llm.at[mine], llm_out.at[mine], loc_sem.at[0])]
    outs[0].start()
    wait_all(opp, xo_sem.at[0], xo_sem.at[1])
    llm[1 - mine] = (opp[...].astype(F32) + text[1 - mine].astype(F32)).astype(BF)
    outs.append(pltpu.make_async_copy(llm.at[1 - mine], llm_out.at[1 - mine], loc_sem.at[1]))
    outs[1].start()
    @pl.when(y < 3)
    def _():
        remote(passing, passing, pool_s.at[4], pool_r.at[4], other).wait_send()

    block = wfull.at[pl.ds(0, 15 * KB)]
    remote(block, block, ws_sem.at[0], wl_sem.at[0], other).wait_send()
    for cp in got_cps:
        cp.wait()
    for cp in outs:
        cp.wait()


def write_kernel(
    row_hbm, got_hbm, llm_hbm, ready_hbm, out_hbm, grad_hbm, row, got, llm, grad, place, in_sem, out_sem
):
    tiles = D // TILE

    def get(i):
        cols = pl.ds(pl.multiple_of(i * TILE, TILE), TILE)
        return pltpu.make_async_copy(got_hbm.at[:, cols], got.at[i], in_sem.at[i])

    def put(i):
        cols = pl.ds(pl.multiple_of(i * TILE, TILE), TILE)
        return pltpu.make_async_copy(grad.at[i], grad_hbm.at[:, cols], out_sem.at[i])

    def put_llm(h):
        return pltpu.make_async_copy(llm.at[h], out_hbm.at[:, pl.ds(h * CW, CW)], out_sem.at[tiles + h])

    row_cp = pltpu.make_async_copy(row_hbm, row, in_sem.at[tiles])
    row_cp.start()
    llm_in = pltpu.make_async_copy(llm_hbm, llm, in_sem.at[tiles + 1])
    for i in range(PRE, tiles):
        get(i).start()
    ready = [pltpu.make_async_copy(ready_hbm.at[i], grad.at[i], in_sem.at[i]) for i in range(PRE)]
    for cp in ready:
        cp.start()
    llm_in.start()
    row_cp.wait()
    vi = lax.broadcasted_iota(jnp.int32, (VROWS, SLOT), 0)
    place[...] = jnp.where(vi == row[0:1, :], 1.0, 0.0).astype(BF)

    def tile(i, c):
        get(i).wait()
        grad[i] = mm(place[...], got[i]).astype(BF)
        put(i).start()
        return c

    lax.fori_loop(PRE, tiles, tile, 0)
    for i in range(PRE):
        ready[i].wait()
        put(i).start()
    llm_in.wait()
    for h in range(NC):
        put_llm(h).start()
    for i in range(tiles):
        put(i).wait()
    for h in range(NC):
        put_llm(h).wait()


def shards(frames, conv_weight, proj_weight, table, audio_pos, token_ids, cotangent):
    relay = relay_matrix()
    consts = [relay, relay.T, channel_matrix(), pack_matrices(), unpack_matrices()]
    consts = [jnp.asarray(m, dtype=BF) for m in consts]
    hbm = pl.BlockSpec(memory_space=pltpu.HBM)
    anywhere = pl.BlockSpec(memory_space=pl.ANY)
    dma = pltpu.SemaphoreType.DMA
    wide = pltpu.VMEM((NC, SLOT, CW), BF)
    llm, got, ready, rows = pl.pallas_call(
        comm_kernel,
        out_shape=[
            jax.ShapeDtypeStruct((NC, SLOT, CW), BF),
            jax.ShapeDtypeStruct((SLOT, D), BF),
            jax.ShapeDtypeStruct((PRE, VROWS, TILE), BF),
            jax.ShapeDtypeStruct((8, SLOT), jnp.int32),
        ],
        in_specs=[hbm] * 12,
        out_specs=[anywhere, anywhere, anywhere, pl.BlockSpec(memory_space=pltpu.VMEM)],
        scratch_shapes=[
            pltpu.VMEM((1, SLOT), jnp.int32),
            pltpu.VMEM((1, RUN), jnp.int32),
            pltpu.VMEM((FR, CH), BF),
            pltpu.VMEM((TAPS, CH), BF),
            pltpu.VMEM((WROWS, D), BF),
            pltpu.VMEM((SLOT, SLOT), BF),
            pltpu.VMEM((SLOT, SLOT), BF),
            pltpu.VMEM((CH, CH), BF),
            pltpu.VMEM((144, 16), BF),
            pltpu.VMEM((240, 128), BF),
            pltpu.VMEM((SLOT, D), BF),
            pltpu.VMEM((VROWS, D), BF),
            pltpu.VMEM((SLOT, SLOT), BF),
            wide, wide, wide, wide, wide, wide, wide, wide,
            pltpu.VMEM((8, 128), jnp.int32),
            pltpu.VMEM((64, 128), jnp.int32),
            pltpu.VMEM((8, 128), jnp.int32),
            pltpu.VMEM((128, 128), jnp.int32),
            pltpu.VMEM((2, 16, CH), BF),
            pltpu.VMEM((5, FR + 32, 128), F32),
            pltpu.VMEM((5, 32, 128), F32),
            pltpu.VMEM((64, 128), F32),
            pltpu.VMEM((RUN, CH), BF),
            pltpu.VMEM((2, RUN, CH), BF),
            pltpu.VMEM((2, RUN, CH), BF),
            pltpu.VMEM((16, D), F32),
            pltpu.VMEM((16, WP), BF),
            pltpu.VMEM((128, WP), BF),
            pltpu.VMEM((NC, KB, CW), BF),
            pltpu.VMEM((PLANE * KB, CW), BF),
            pltpu.VMEM((2, 2 * SLOT, CH), BF),
            pltpu.VMEM((SLOT, CW), BF),
            pltpu.VMEM((SLOT, CW), BF),
            wide, wide,
            pltpu.VMEM((PART, CH), BF),
            pltpu.VMEM((VROWS, SLOT), BF),
            pltpu.VMEM((PRE, VROWS, TILE), BF),
            pltpu.VMEM((SLOT, D), BF),
            dma((12,)), dma((2,)), dma((2,)), dma((2,)), dma((7,)),
            dma((2, 2, 2)), dma((2, 2)), dma((2, 2, 2)), dma((2, 2)),
            dma((1,)), dma((4,)), dma((2, 4)), dma((2,)), dma((5,)), dma((5,)), dma((2,)), dma((2,)),
        ],
        compiler_params=pltpu.CompilerParams(
            collective_id=0, has_side_effects=True, vmem_limit_bytes=VMEM_LIMIT
        ),
        name="exchange",
    )(
        token_ids.reshape(1, SLOT), audio_pos.reshape(1, RUN), frames, conv_weight, proj_weight, *consts,
        cotangent, table,
    )
    return pl.pallas_call(
        write_kernel,
        out_shape=[jax.ShapeDtypeStruct((SLOT, D), BF), jax.ShapeDtypeStruct((VROWS, D), BF)],
        in_specs=[hbm] * 4,
        out_specs=[anywhere, anywhere],
        scratch_shapes=[
            pltpu.VMEM((8, SLOT), jnp.int32),
            pltpu.VMEM((D // TILE, SLOT, TILE), BF),
            wide,
            pltpu.VMEM((D // TILE, VROWS, TILE), BF),
            pltpu.VMEM((VROWS, SLOT), BF),
            dma((D // TILE + 2,)),
            dma((D // TILE + 2,)),
        ],
        compiler_params=pltpu.CompilerParams(vmem_limit_bytes=VMEM_LIMIT),
        name="write",
    )(rows, got, llm, ready)


def solution(mesh):
    return jax.shard_map(
        shards,
        mesh=mesh,
        in_specs=(
            P("seq", "vocab"),
            P(None, "vocab"),
            P("seq", "vocab"),
            P("seq", "vocab"),
            P("seq"),
            P("seq"),
            P("seq", "vocab"),
        ),
        out_specs=(P("seq", "vocab"), P("seq", "vocab")),
        check_vma=False,
    )
```
